32 devices in a mesh: group: 4 (over y, core), dev: 8 (over z, x).
Axes of the slice: x: 2, y: 2, z: 4, core: 2. Of those that a mesh axis runs over, the one named last changes fastest.
Arguments:
- queries: bfloat16 [3072, 1024], P(('group', 'dev')), may hold values from -12 to 12
- keys: bfloat16 [128, 256, 1024], P(('group', 'dev')), may hold values from -12 to 12
- values: bfloat16 [128, 256, 1024], P(('group', 'dev')), may hold values from -6 to 6
- frame_slot: int32 [128], replicated, may hold values from 0 to 127, each once
- covisible: int32 [12, 40], replicated, may hold values from 0 to 127, as said below
- counts: int32 [12], replicated, may hold values from 4 to 40
- out_weight: bfloat16 [1024, 1024], replicated, may hold values from -0.1875 to 0.1875
Outputs:
- projected: bfloat16 [3072, 1024], P(('group', 'dev'))
The draws below stay inside these ranges and needn't reach their ends.
Inputs may be any that keep to these rules, and one draw needn't show every extreme that they name: `covisible`: each row lists 40 different frame numbers; query frame q attends to the first counts[q] of them. `frame_slot`: every frame is held at exactly one storage row.
All inputs are finite; a program needn't handle non-finite values.
Results may differ from the reference program's by a relative error of at most 0.02.
Values may be sent and summed in bfloat16 or wider, within the bound.
A program may use at most 192 MiB of HBM per device.

```python
import jax
import jax.numpy as jnp
from jax import lax

D = 1024
HEADS = 16
HD = 64
TOK = 256
QF = 12
FRAMES = 128
MAXCOV = 40
MINCOV = 4


def covisible_lists(key):
    base = jax.random.fold_in(key, 202)
    first, second, third, fourth, fifth = jax.random.split(base, 5)
    centers = jax.random.randint(first, (QF,), 0, FRAMES // 4)
    offsets = jax.vmap(lambda piece: jax.random.permutation(piece, 2 * MAXCOV))(jax.random.split(second, QF))
    lists = (centers[:, None] + offsets[:, :MAXCOV] - MAXCOV) % FRAMES
    used = jax.random.randint(third, (QF,), MINCOV, MAXCOV + 1)
    top_row = jax.random.randint(fourth, (), 0, QF)
    low_row = (top_row + 1 + jax.random.randint(fifth, (), 0, QF - 1)) % QF
    used = used.at[top_row].set(MAXCOV).at[low_row].set(MINCOV)
    return (lists.astype(jnp.int32), used.astype(jnp.int32))


def draw_covisible(key, part):
    return covisible_lists(key)[0]


def draw_counts(key, part):
    return covisible_lists(key)[1]


def draw_keys(key, part):
    key = jax.random.fold_in(key, 3)
    first = jax.random.fold_in(key, 0)
    result = jax.random.normal(first, (FRAMES, TOK, D), jnp.float32)
    return jnp.clip(result, -12.0, 12.0).astype(jnp.bfloat16)


def draw_queries(key, part):
    key = jax.random.fold_in(key, 4)
    first = jax.random.fold_in(key, 0)
    result = jax.random.normal(first, (QF, TOK, D), jnp.float32)
    return jnp.clip(result, -12.0, 12.0).reshape(QF * TOK, D).astype(jnp.bfloat16)


def levels(own_key, shape, cuts, smallest, top_value):
    loudness, own = 1.0, jax.random.fold_in(own_key, 6)
    for axis_at, parts in cuts:
        steps = jnp.exp(jax.random.uniform(jax.random.fold_in(own, axis_at), (parts,), jnp.float32, smallest / len(cuts), top_value / len(cuts)))
        loudness = loudness * jnp.repeat(steps, shape[axis_at] // parts).reshape([-1 if axis == axis_at else 1 for axis in range(len(shape))])
    return loudness


def bell_draw(rng, shape, deviation, limit, pieces=(), held_as=jnp.bfloat16):
    entries = jax.random.normal(rng, shape, jnp.float32) * deviation
    if len(pieces) > 0:
        entries = levels(rng, shape, pieces, -0.22, 0.18) * entries
    return jnp.clip(entries, min=-limit, max=limit).astype(held_as)


def setup_inputs(seed: int = 0) -> dict:
    arg_keys = jax.random.split(jax.random.key(seed), 8)
    return {
        "queries": draw_queries(jax.random.fold_in(arg_keys[7], 71), 0),
        "keys": draw_keys(jax.random.fold_in(arg_keys[7], 71), 0),
        "values": bell_draw(arg_keys[2], (FRAMES, TOK, D), 1.0, 6.0, ((0, 32),)),
        "frame_slot": jax.random.permutation(arg_keys[3], FRAMES).astype(jnp.int32),
        "covisible": draw_covisible(jax.random.fold_in(arg_keys[7], 71), 0),
        "counts": draw_counts(jax.random.fold_in(arg_keys[7], 71), 0),
        "out_weight": bell_draw(arg_keys[6], (D, D), D ** -0.5, 0.1875),
    }


NEG_FILL = -1.0e30
LOG2E = 1.4426950408889634


def reference(queries, keys, values, frame_slot, covisible, counts, out_weight):
    score_scale = HD ** -0.5
    query_heads = queries.reshape(QF, TOK, HEADS, HD).astype(jnp.float32)

    def one_frame(packed):
        query_rows, frame_list, used = packed
        slot_list = jnp.take(frame_slot, frame_list).astype(jnp.int32)

        def frame_scores(position):
            slot_index = slot_list[position]
            key_rows = lax.dynamic_index_in_dim(keys, slot_index, 0, keepdims=False)
            key_rows = key_rows.reshape(TOK, HEADS, HD).astype(jnp.float32)
            return jnp.einsum("rhd,khd->rhk", query_rows, key_rows) * score_scale

        def max_step(running, position):
            maxima = jnp.max(frame_scores(position), axis=2)
            return jnp.where(position < used, jnp.maximum(running, maxima), running), None

        start_top = jnp.full((TOK, HEADS), NEG_FILL, jnp.float32)
        raw_top, _ = lax.scan(max_step, start_top, jnp.arange(MAXCOV, dtype=jnp.int32))
        row_top = jnp.ceil(raw_top * LOG2E)

        def sum_step(carry, position):
            numer, totals = carry
            weights = jnp.exp2(frame_scores(position) * LOG2E - row_top[:, :, None])
            weights = jnp.where(position < used, weights, jnp.float32(0.0))
            rounded = lax.optimization_barrier(weights.astype(jnp.bfloat16)).astype(jnp.float32)
            value_rows = lax.dynamic_index_in_dim(values, slot_list[position], 0, keepdims=False)
            value_rows = value_rows.reshape(TOK, HEADS, HD).astype(jnp.float32)
            numer = numer + jnp.einsum("rhk,khd->rhd", rounded, value_rows)
            totals = totals + jnp.sum(weights, axis=2)
            return (numer, totals), None

        start = (jnp.zeros((TOK, HEADS, HD), jnp.float32), jnp.zeros((TOK, HEADS), jnp.float32))
        (numer, totals), _ = lax.scan(sum_step, start, jnp.arange(MAXCOV, dtype=jnp.int32))
        return (numer / totals[:, :, None]).reshape(TOK, D).astype(jnp.bfloat16)

    attended = lax.map(one_frame, (query_heads, covisible, counts))
    attended = attended.reshape(QF * TOK, D)
    return jnp.dot(attended, out_weight, preferred_element_type=jnp.float32).astype(jnp.bfloat16)
```

```python
import functools

import jax
import jax.numpy as jnp
from jax import lax
from jax.experimental import pallas as pl
from jax.experimental.pallas import tpu as pltpu
from jax.sharding import PartitionSpec as P

HD = 64
NEG_FILL = -1e30
LOG2E = 1.4426950408889634
MESH = pl.DeviceIdType.MESH
STAT = 128
TOP_STEP = 8.0
VMEM_LIMIT = 56 * 1024 * 1024


def attend_kernel(flags, q_ref, k_ref, v_ref, out_ref, vt, qm, acc, stat, *, heads, frames, tok, qframes):
    width = heads * HD
    scale = LOG2E * HD ** (-0.5)

    def turn(f, carry):
        turned = v_ref[f].astype(jnp.float32).T.astype(jnp.bfloat16)
        for h in range(heads):
            vt[f, h, 0:HD, :] = turned[h * HD : (h + 1) * HD, :]
            vt[f, h, HD : HD + 16, :] = jnp.ones((16, tok), jnp.bfloat16)
        return carry

    lax.fori_loop(0, frames, turn, 0)
    lane = lax.broadcasted_iota(jnp.int32, (tok, 128), 1)
    low = jnp.where(lane < HD, 1.0, 0.0).astype(jnp.bfloat16)
    high = jnp.where(lane < HD, 0.0, 1.0).astype(jnp.bfloat16)
    stat[...] = jnp.zeros_like(stat)

    def one_query(qi, carry):
        rows = pl.ds(pl.multiple_of(qi * tok, tok), tok)
        for h in range(heads):
            pair = q_ref[rows, (h // 2) * 128 : (h // 2 + 1) * 128]
            qm[h] = pair * (low if h % 2 == 0 else high)
        acc[...] = jnp.zeros_like(acc)
        stat[0:heads, :] = jnp.full((heads, tok), NEG_FILL, jnp.float32)

        def one_frame(f, c):
            @pl.when(flags[qi * frames + f] != 0)
            def _():
                for h in range(heads):
                    kp = k_ref[f, :, (h // 2) * 128 : (h // 2 + 1) * 128]
                    s = lax.dot_general(
                        kp, qm[h], (((1,), (1,)), ((), ())), preferred_element_type=jnp.float32
                    )
                    top = jnp.max(s, axis=0, keepdims=True) * scale
                    old = stat[h : h + 1, :]
                    new = jnp.maximum(old, jnp.ceil(top * (1.0 / TOP_STEP)) * TOP_STEP)
                    p = jnp.exp2(s * scale - new).astype(jnp.bfloat16)
                    add = jnp.dot(vt[f, h], p, preferred_element_type=jnp.float32)
                    acc[h] = acc[h] * jnp.exp2(old - new) + add
                    stat[h : h + 1, :] = new

            return c

        lax.fori_loop(0, frames, one_frame, 0)
        for h in range(heads):
            stat[heads + h : heads + h + 1, :] = acc[h, HD : HD + 1, :]
        for g in range(heads // 2):
            both = jnp.concatenate([acc[2 * g, 0:HD, :], acc[2 * g + 1, 0:HD, :]], axis=0)
            out_ref[rows, g * 128 : (g + 1) * 128] = both.T.astype(jnp.bfloat16)
        out_ref[rows, width : width + STAT] = stat[...].T.astype(jnp.bfloat16)
        return carry

    lax.fori_loop(0, qframes, one_query, 0)


def attend(flags, q, k, v):
    rows, width = q.shape
    frames, tok = k.shape[0], k.shape[1]
    heads = width // HD
    qframes = rows // tok
    return pl.pallas_call(
        functools.partial(attend_kernel, heads=heads, frames=frames, tok=tok, qframes=qframes),
        out_shape=jax.ShapeDtypeStruct((rows, width + STAT), jnp.bfloat16),
        in_specs=[pl.BlockSpec(memory_space=pltpu.SMEM)] + [pl.BlockSpec(memory_space=pltpu.VMEM)] * 3,
        out_specs=pl.BlockSpec(memory_space=pltpu.VMEM),
        scratch_shapes=[
            pltpu.VMEM((frames, heads, HD + 16, tok), jnp.bfloat16),
            pltpu.VMEM((heads, tok, 128), jnp.bfloat16),
            pltpu.VMEM((heads, HD + 16, tok), jnp.float32),
            pltpu.VMEM((STAT, tok), jnp.float32),
        ],
        compiler_params=pltpu.CompilerParams(vmem_limit_bytes=VMEM_LIMIT),
        name="attend",
    )(flags, q, k, v)


class Place:
    def __init__(self, nz):
        g, d = lax.axis_index("group"), lax.axis_index("dev")
        self.nz = nz
        self.y, self.c = lax.div(g, 2), lax.rem(g, 2)
        self.z, self.x = lax.div(d, 2), lax.rem(d, 2)
        self.other = (self.y * 2 + 1 - self.c, d)
        self.over_x = (g, self.z * 2 + 1 - self.x)
        self.over_y = ((1 - self.y) * 2 + self.c, d)
        self.up = (g, (self.z + 1) * 2 + self.x)
        self.down = (g, (self.z - 1) * 2 + self.x)
        self.has_up = self.z + 1 < nz
        self.has_down = self.z > 0

    def owner(self, p, x, y, z):
        return ((y * 2 + p) * self.nz + z) * 2 + x

    def greet(self):
        barrier = pltpu.get_barrier_semaphore()

        def tell(to):
            pl.semaphore_signal(barrier, inc=1, device_id=to, device_id_type=MESH)

        tell(self.other)
        tell(self.over_x)
        tell(self.over_y)
        pl.when(self.has_up)(lambda: tell(self.up))
        pl.when(self.has_down)(lambda: tell(self.down))
        peers = 3 + jnp.where(self.has_up, 1, 0) + jnp.where(self.has_down, 1, 0)
        pl.semaphore_wait(barrier, peers)


def remote(src, dst, send, recv, to):
    return pltpu.make_async_remote_copy(
        src_ref=src, dst_ref=dst, send_sem=send, recv_sem=recv, device_id=to, device_id_type=MESH
    )


def gather_kernel(
    q_in, k_in, v_in, q_all, k_all, v_all, arrive, s_up, s_down, s_x, s_y, s_two, s_near, r_near, s_own, *, nz
):
    me = Place(nz)
    half = q_all.shape[2]
    here = k_in.shape[0]
    keep = pl.ds(pl.multiple_of(me.c * half, half), half)
    give = pl.ds(pl.multiple_of((1 - me.c) * half, half), half)
    mine = pl.ds(me.c * here, here)
    theirs = pl.ds((1 - me.c) * here, here)
    own = me.owner(me.c, me.x, me.y, me.z)
    own_copies = [
        pltpu.make_async_copy(q_in.at[:, keep], q_all.at[own], s_own.at[0]),
        pltpu.make_async_copy(k_in.at[:, :, keep], k_all.at[mine], s_own.at[1]),
        pltpu.make_async_copy(v_in.at[:, :, keep], v_all.at[mine], s_own.at[2]),
    ]
    own_copies[0].start()
    me.greet()
    near_q = remote(q_in.at[:, give], q_all.at[own], s_near.at[0], arrive.at[own], me.other)
    near_k = remote(k_in.at[:, :, give], k_all.at[mine], s_near.at[1], r_near.at[0], me.other)
    near_v = remote(v_in.at[:, :, give], v_all.at[mine], s_near.at[2], r_near.at[1], me.other)
    near_q.start()
    own_copies[0].wait()

    def await_block(idx):
        remote(q_all.at[idx], q_all.at[idx], s_near.at[0], arrive.at[idx], me.over_x).wait_recv()

    def spread(p, i, off, zs):
        idx = me.owner(p, me.x, me.y, zs)
        blk = q_all.at[idx]
        up = remote(blk, blk, s_up.at[p, i], arrive.at[idx], me.up)
        down = remote(blk, blk, s_down.at[p, i], arrive.at[idx], me.down)
        return (
            (jnp.logical_and(off >= 0, me.has_up), up),
            (jnp.logical_and(off <= 0, me.has_down), down),
            (None, remote(blk, blk, s_x.at[p, i], arrive.at[idx], me.over_x)),
            (None, remote(blk, blk, s_y.at[p, i], arrive.at[idx], me.over_y)),
        )

    def begin(copies):
        for cond, copy in copies:
            if cond is None:
                copy.start()
            else:
                pl.when(cond)(copy.start)

    def sent(copies):
        for cond, copy in copies:
            if cond is None:
                copy.wait_send()
            else:
                pl.when(cond)(copy.wait_send)

    begin(spread(me.c, 0, jnp.int32(0), me.z))
    await_block(me.owner(1 - me.c, me.x, me.y, me.z))
    begin(spread(1 - me.c, 0, jnp.int32(0), me.z))
    near_k.start()
    near_v.start()
    own_copies[1].start()
    own_copies[2].start()

    def source(i):
        off = lax.div(i + 1, 2) * (2 * lax.rem(i, 2) - 1)
        zs = me.z - off
        return off, zs, jnp.logical_and(zs >= 0, zs < nz)

    def second(i, zs):
        a = me.owner(0, 1 - me.x, me.y, zs)
        b = me.owner(1, me.x, 1 - me.y, zs)
        return (
            (a, remote(q_all.at[a], q_all.at[a], s_two.at[0, i], arrive.at[a], me.over_y)),
            (b, remote(q_all.at[b], q_all.at[b], s_two.at[1, i], arrive.at[b], me.over_x)),
        )

    def do_second(i):
        off, zs, ok = source(i)

        @pl.when(ok)
        def _():
            for idx, copy in second(i, zs):
                await_block(idx)
                copy.start()

    def step(i, carry):
        off, zs, ok = source(i)

        @pl.when(ok)
        def _():
            for p in (0, 1):
                await_block(me.owner(p, me.x, me.y, zs))
                begin(spread(p, i, off, zs))

        do_second(i - 1)
        return carry

    count = 2 * nz - 1
    lax.fori_loop(1, count, step, 0)
    do_second(jnp.int32(count - 1))

    def finish(i, carry):
        off, zs, ok = source(i)

        @pl.when(ok)
        def _():
            await_block(me.owner(0, me.x, 1 - me.y, zs))
            await_block(me.owner(1, 1 - me.x, me.y, zs))
            await_block(me.owner(0, 1 - me.x, 1 - me.y, zs))
            await_block(me.owner(1, 1 - me.x, 1 - me.y, zs))
            for p in (0, 1):
                sent(spread(p, i, off, zs))
            for _, copy in second(i, zs):
                copy.wait_send()

        return carry

    lax.fori_loop(0, count, finish, 0)
    near_q.wait_send()
    for near, full in ((near_k, k_all), (near_v, v_all)):
        near.wait_send()
        near.wait_recv()
    own_copies[1].wait()
    own_copies[2].wait()


def gather(q, k, v, devices):
    rows, width = q.shape
    frames, tok, _ = k.shape
    nz = devices // 8
    half = width // 2
    count = 2 * nz - 1
    dma = pltpu.SemaphoreType.DMA
    anywhere = pl.BlockSpec(memory_space=pl.ANY)
    return pl.pallas_call(
        functools.partial(gather_kernel, nz=nz),
        out_shape=(
            jax.ShapeDtypeStruct((devices, rows, half), q.dtype),
            jax.ShapeDtypeStruct((2 * frames, tok, half), k.dtype),
            jax.ShapeDtypeStruct((2 * frames, tok, half), v.dtype),
        ),
        in_specs=[anywhere] * 3,
        out_specs=(anywhere,) * 3,
        scratch_shapes=[
            dma((devices,)),
            dma((2, count)),
            dma((2, count)),
            dma((2, count)),
            dma((2, count)),
            dma((2, count)),
            dma((3,)),
            dma((2,)),
            dma((3,)),
        ],
        compiler_params=pltpu.CompilerParams(
            collective_id=0, has_side_effects=True, vmem_limit_bytes=VMEM_LIMIT
        ),
        name="gather",
    )(q, k, v)


def expander(heads, first, width):
    r = lax.broadcasted_iota(jnp.int32, (STAT, width), 0)
    col = lax.broadcasted_iota(jnp.int32, (STAT, width), 1)
    head = jnp.where(col < heads * HD, lax.div(col, HD), col - heads * HD - heads)
    head = jnp.where(head < 0, -STAT, jnp.where(head < heads, head, -STAT))
    return jnp.where(head + first == r, 1.0, 0.0).astype(jnp.bfloat16)


def scatter_kernel(
    msg, out, r_one, r_two, r_up, r_down, b_two, b_z, kept, att, exp_ref, exp_tot,
    sem_one, sem_two, sem_up, sem_down, s_one, s_two, s_z, sem_last, *, nz, heads
):
    me = Place(nz)
    width = heads * HD
    rows = msg.shape[1]
    count = 2 * nz - 1
    exp_ref[...] = expander(heads, 0, width + STAT)
    exp_tot[...] = expander(heads, heads, width)
    me.greet()
    lane = lax.broadcasted_iota(jnp.int32, (rows, STAT), 1)

    def target(i):
        off = lax.div(count - i, 2) * (1 - 2 * lax.rem(i, 2))
        zd = me.z + off
        return off, zd, jnp.logical_and(zd >= 0, zd < nz)

    def merge(parts):
        parts = [part.astype(jnp.float32) for part in parts]
        stats = [part[:, width:] for part in parts]
        top = functools.reduce(jnp.maximum, stats)
        total = None
        for part, st in zip(parts, stats):
            factor = jnp.exp2(st - top).astype(jnp.bfloat16)
            wide = jnp.dot(factor, exp_ref[...], preferred_element_type=jnp.float32)
            total = part * wide if total is None else total + part * wide
        tail = jnp.where(lane < heads, top, total[:, width:])
        return jnp.concatenate([total[:, :width], tail], axis=1)

    def ones(i, zd):
        a0 = me.owner(0, 1 - me.x, 1 - me.y, zd)
        a1 = me.owner(0, me.x, 1 - me.y, zd)
        b0 = me.owner(1, 1 - me.x, 1 - me.y, zd)
        b1 = me.owner(1, 1 - me.x, me.y, zd)
        return tuple(
            remote(msg.at[src], r_one.at[p, k, zd], s_one.at[p, k, zd], sem_one.at[p, k, zd], to)
            for p, k, src, to in (
                (0, 0, a0, me.over_y), (1, 0, b0, me.over_x), (0, 1, a1, me.over_y), (1, 1, b1, me.over_x)
            )
        )

    def first(i, carry):
        off, zd, ok = target(i)

        @pl.when(ok)
        def _():
            for copy in ones(i, zd):
                copy.start()

        return carry

    lax.fori_loop(0, count, first, 0)

    def twos(zd):
        return tuple(
            remote(b_two.at[p, zd], r_two.at[p, zd], s_two.at[p, zd], sem_two.at[p, zd], to)
            for p, to in ((0, me.over_x), (1, me.over_y))
        )

    def second(i):
        off, zd, ok = target(i)

        @pl.when(ok)
        def _():
            waits = ones(i, zd)
            copies = twos(zd)
            for p in (0, 1):
                waits[p].wait_recv()
                src = me.owner(0, 1 - me.x, me.y, zd) if p == 0 else me.owner(1, me.x, 1 - me.y, zd)
                b_two[p, zd] = merge([msg[src], r_one[p, 0, zd]]).astype(jnp.bfloat16)
                copies[p].start()

    def z_copies(p, zd):
        return (
            remote(b_z.at[p, zd], r_up.at[p, zd], s_z.at[p, zd], sem_up.at[p, zd], me.up),
            remote(b_z.at[p, zd], r_down.at[p, zd], s_z.at[p, zd], sem_down.at[p, zd], me.down),
        )

    def third(i):
        off, zd, ok = target(i)

        @pl.when(ok)
        def _():
            waits = ones(i, zd)
            two = twos(zd)
            for p in (0, 1):
                up, down = z_copies(p, zd)
                waits[2 + p].wait_recv()
                two[p].wait_recv()
                here = merge([msg[me.owner(p, me.x, me.y, zd)], r_one[p, 1, zd], r_two[p, zd]])
                kept[p] = here

                @pl.when(jnp.logical_and(off >= 0, me.has_down))
                def _():
                    up.wait_recv()
                    kept[p] = merge([kept[p], r_up[p, zd]])

                @pl.when(jnp.logical_and(off <= 0, me.has_up))
                def _():
                    down.wait_recv()
                    kept[p] = merge([kept[p], r_down[p, zd]])

                @pl.when(off != 0)
                def _():
                    b_z[p, zd] = kept[p].astype(jnp.bfloat16)

                pl.when(off > 0)(up.start)
                pl.when(off < 0)(down.start)

    def step(i, carry):
        second(i)
        pl.when(i > 0)(lambda: third(i - 1))
        return carry

    lax.fori_loop(0, count, step, 0)
    third(jnp.int32(count - 1))

    for p in (0, 1):
        full = kept[p]
        tail = full[:, width:]
        inverse = 1.0 / jnp.where(jnp.logical_and(lane >= heads, lane < 2 * heads), tail, 1.0)
        hi = inverse.astype(jnp.bfloat16)
        lo = (inverse - hi.astype(jnp.float32)).astype(jnp.bfloat16)
        wide = jnp.dot(hi, exp_tot[...], preferred_element_type=jnp.float32)
        wide = wide + jnp.dot(lo, exp_tot[...], preferred_element_type=jnp.float32)
        att[p] = (full[:, :width] * wide).astype(jnp.bfloat16)
    last = remote(att.at[1 - me.c], out.at[me.c], sem_last.at[0], sem_last.at[1], me.other)
    last.start()
    out[me.c] = att[me.c]

    def finish(i, carry):
        off, zd, ok = target(i)

        @pl.when(ok)
        def _():
            for copy in ones(i, zd):
                copy.wait_send()
            for copy in twos(zd):
                copy.wait_send()
            for p in (0, 1):
                up, down = z_copies(p, zd)
                pl.when(off > 0)(up.wait_send)
                pl.when(off < 0)(down.wait_send)

        return carry

    lax.fori_loop(0, count, finish, 0)
    last.wait()


def scatter(msg, heads):
    devices, rows, wide = msg.shape
    nz = devices // 8
    width = heads * HD
    dma = pltpu.SemaphoreType.DMA
    vmem = pl.BlockSpec(memory_space=pltpu.VMEM)
    block = (rows, wide)
    return pl.pallas_call(
        functools.partial(scatter_kernel, nz=nz, heads=heads),
        out_shape=jax.ShapeDtypeStruct((2, rows, width), jnp.bfloat16),
        in_specs=[vmem],
        out_specs=vmem,
        scratch_shapes=[
            pltpu.VMEM((2, 2, nz) + block, jnp.bfloat16),
            pltpu.VMEM((2, nz) + block, jnp.bfloat16),
            pltpu.VMEM((2, nz) + block, jnp.bfloat16),
            pltpu.VMEM((2, nz) + block, jnp.bfloat16),
            pltpu.VMEM((2, nz) + block, jnp.bfloat16),
            pltpu.VMEM((2, nz) + block, jnp.bfloat16),
            pltpu.VMEM((2,) + block, jnp.float32),
            pltpu.VMEM((2, rows, width), jnp.bfloat16),
            pltpu.VMEM((STAT, wide), jnp.bfloat16),
            pltpu.VMEM((STAT, width), jnp.bfloat16),
            dma((2, 2, nz)),
            dma((2, nz)),
            dma((2, nz)),
            dma((2, nz)),
            dma((2, 2, nz)),
            dma((2, nz)),
            dma((2, nz)),
            dma((2,)),
        ],
        compiler_params=pltpu.CompilerParams(
            collective_id=1, has_side_effects=True, vmem_limit_bytes=VMEM_LIMIT
        ),
        name="scatter",
    )(msg)


def needed_frames(rows, frame_slot, covisible, counts):
    frame_ids = jnp.arange(frame_slot.shape[0], dtype=jnp.int32)
    hits = frame_slot[None, :] == rows[:, None]
    frames = jnp.sum(jnp.where(hits, frame_ids[None, :], 0), axis=1)
    in_list = jnp.arange(covisible.shape[1], dtype=jnp.int32)[None, :] < counts[:, None]
    match = (covisible[:, :, None] == frames[None, None, :]) & in_list[:, :, None]
    return jnp.any(match, axis=1).astype(jnp.int32)


def body_cores(devices, per_group, queries, keys, values, frame_slot, covisible, counts, out_weight):
    here, tok, width = keys.shape
    heads = width // HD // 2
    g, d = lax.axis_index("group"), lax.axis_index("dev")
    base = (lax.div(g, 2) * 2 * per_group + d) * here
    rows = jnp.arange(here, dtype=jnp.int32) + base
    rows = jnp.concatenate([rows, rows + per_group * here])
    flags = needed_frames(rows, frame_slot, covisible, counts).reshape(-1)
    q_all, k_all, v_all = gather(queries, keys, values, devices)
    own = queries.shape[0]
    msg = attend(flags, q_all.reshape(devices * own, width // 2), k_all, v_all)
    halves = scatter(msg.reshape(devices, own, -1), heads)
    weight = out_weight.reshape(2, width // 2, -1)
    return jnp.einsum("hrd,hde->re", halves, weight, preferred_element_type=jnp.float32).astype(jnp.bfloat16)


def body_any(queries, keys, values, frame_slot, covisible, counts, out_weight):
    axes = ("group", "dev")
    here, tok, width = keys.shape
    heads = width // HD
    rows = jnp.arange(here, dtype=jnp.int32) + lax.axis_index(axes) * here
    flags = needed_frames(rows, frame_slot, covisible, counts).reshape(-1)
    q_all = lax.all_gather(queries, axes, axis=0, tiled=True)
    msg = attend(flags, q_all, keys, values).astype(jnp.float32)
    top = msg[:, width : width + heads]
    totals = msg[:, width + heads : width + 2 * heads]
    factor = jnp.exp2(top - lax.pmax(top, axes))
    numer = msg[:, :width] * jnp.repeat(factor, HD, axis=1)
    own_numer = lax.psum_scatter(numer, axes, scatter_dimension=0, tiled=True)
    own_totals = lax.psum_scatter(totals * factor, axes, scatter_dimension=0, tiled=True)
    attended = (own_numer / jnp.repeat(own_totals, HD, axis=1)).astype(jnp.bfloat16)
    return jnp.dot(attended, out_weight, preferred_element_type=jnp.float32).astype(jnp.bfloat16)


def solution(mesh):
    group, dev = mesh.shape["group"], mesh.shape["dev"]
    body = body_any
    if group == 4 and dev % 2 == 0:
        body = functools.partial(body_cores, group * dev, dev)
    return jax.shard_map(
        body,
        mesh=mesh,
        in_specs=(
            P(("group", "dev"), None),
            P(("group", "dev"), None, None),
            P(("group", "dev"), None, None),
            P(),
            P(),
            P(),
            P(),
        ),
        out_specs=P(("group", "dev"), None),
        check_vma=False,
    )
```

```python
import functools

import jax
import jax.numpy as jnp
from jax import lax
from jax.experimental import pallas as pl
from jax.experimental.pallas import tpu as pltpu
from jax.sharding import PartitionSpec as P

HD = 64
NEG_FILL = -1e30
LOG2E = 1.4426950408889634
MESH = pl.DeviceIdType.MESH
STAT = 128
TOP_STEP = 8.0
SMALL = 60.0
VMEM_LIMIT = 56 * 1024 * 1024


def attend_kernel(flags, q_ref, k_ref, v_ref, out_ref, vt, qt, acc, stat, *, heads, frames, tok, qframes):
    width = heads * HD
    scale = LOG2E * HD ** (-0.5)

    row_id = lax.broadcasted_iota(jnp.int32, (width, 128), 0)
    col_id = lax.broadcasted_iota(jnp.int32, (width, 128), 1)
    by_head = jnp.where(lax.div(row_id, HD) == col_id, 1.0, 0.0).astype(jnp.bfloat16)

    def largest_square(block):
        squares = jnp.dot(block * block, by_head, preferred_element_type=jnp.float32)
        return jnp.max(squares, axis=0, keepdims=True)

    def turn(f, largest):
        turned = v_ref[f].astype(jnp.float32).T.astype(jnp.bfloat16)
        for h in range(heads):
            vt[f, h, 0:HD, :] = turned[h * HD : (h + 1) * HD, :]
            vt[f, h, HD : HD + 16, :] = jnp.ones((16, tok), jnp.bfloat16)
        return jnp.maximum(largest, largest_square(k_ref[f]))

    key_square = lax.fori_loop(0, frames, turn, jnp.zeros((1, 128), jnp.float32))
    stat[...] = jnp.zeros_like(stat)
    qt[...] = jnp.zeros_like(qt)

    def one_query(qi, carry):
        rows = pl.ds(pl.multiple_of(qi * tok, tok), tok)
        for g in range(heads // 2):
            pair = q_ref[rows, g * 128 : (g + 1) * 128].astype(jnp.float32).T.astype(jnp.bfloat16)
            qt[2 * g, 0:HD, :] = pair[0:HD, :]
            qt[2 * g + 1, HD:128, :] = pair[HD:128, :]
        acc[...] = jnp.zeros_like(acc)
        stat[0:heads, :] = jnp.full((heads, tok), NEG_FILL, jnp.float32)
        bound = jnp.max(largest_square(q_ref[rows, :]) * key_square) * (scale * scale)
        small = bound <= SMALL * SMALL

        def scores(f, h):
            kp = k_ref[f, :, (h // 2) * 128 : (h // 2 + 1) * 128]
            return jnp.dot(kp, qt[h], preferred_element_type=jnp.float32)

        def small_frame(f):
            stat[0:heads, :] = jnp.zeros((heads, tok), jnp.float32)
            s = scores(f, 0)
            for h in range(heads):
                later = scores(f, h + 1) if h + 1 < heads else None
                p = jnp.exp2(s * scale).astype(jnp.bfloat16)
                acc[h] += jnp.dot(vt[f, h], p, preferred_element_type=jnp.float32)
                s = later

        def any_frame(f):
            for h in range(heads):
                s = scores(f, h)
                top = jnp.max(s, axis=0, keepdims=True) * scale
                old = stat[h : h + 1, :]
                new = jnp.maximum(old, jnp.ceil(top * (1.0 / TOP_STEP)) * TOP_STEP)
                p = jnp.exp2(s * scale - new).astype(jnp.bfloat16)
                add = jnp.dot(vt[f, h], p, preferred_element_type=jnp.float32)
                acc[h] = acc[h] * jnp.exp2(old - new) + add
                stat[h : h + 1, :] = new

        def one_frame(f, c):
            needed = flags[qi * frames + f] != 0
            pl.when(jnp.logical_and(needed, small))(lambda: small_frame(f))
            pl.when(jnp.logical_and(needed, jnp.logical_not(small)))(lambda: any_frame(f))
            return c

        lax.fori_loop(0, frames, one_frame, 0)
        for h in range(heads):
            stat[heads + h : heads + h + 1, :] = acc[h, HD : HD + 1, :]
        for g in range(heads // 2):
            both = jnp.concatenate([acc[2 * g, 0:HD, :], acc[2 * g + 1, 0:HD, :]], axis=0)
            out_ref[rows, g * 128 : (g + 1) * 128] = both.T.astype(jnp.bfloat16)
        out_ref[rows, width : width + STAT] = stat[...].T.astype(jnp.bfloat16)
        return carry

    lax.fori_loop(0, qframes, one_query, 0)


def attend(flags, q, k, v):
    rows, width = q.shape
    frames, tok = k.shape[0], k.shape[1]
    heads = width // HD
    qframes = rows // tok
    return pl.pallas_call(
        functools.partial(attend_kernel, heads=heads, frames=frames, tok=tok, qframes=qframes),
        out_shape=jax.ShapeDtypeStruct((rows, width + STAT), jnp.bfloat16),
        in_specs=[pl.BlockSpec(memory_space=pltpu.SMEM)] + [pl.BlockSpec(memory_space=pltpu.VMEM)] * 3,
        out_specs=pl.BlockSpec(memory_space=pltpu.VMEM),
        scratch_shapes=[
            pltpu.VMEM((frames, heads, HD + 16, tok), jnp.bfloat16),
            pltpu.VMEM((heads, 128, tok), jnp.bfloat16),
            pltpu.VMEM((heads, HD + 16, tok), jnp.float32),
            pltpu.VMEM((STAT, tok), jnp.float32),
        ],
        compiler_params=pltpu.CompilerParams(vmem_limit_bytes=VMEM_LIMIT),
        name="attend",
    )(flags, q, k, v)


class Place:
    def __init__(self, nz):
        g, d = lax.axis_index("group"), lax.axis_index("dev")
        self.nz = nz
        self.y, self.c = lax.div(g, 2), lax.rem(g, 2)
        self.z, self.x = lax.div(d, 2), lax.rem(d, 2)
        self.other = (self.y * 2 + 1 - self.c, d)
        self.over_x = (g, self.z * 2 + 1 - self.x)
        self.over_y = ((1 - self.y) * 2 + self.c, d)
        self.up = (g, (self.z + 1) * 2 + self.x)
        self.down = (g, (self.z - 1) * 2 + self.x)
        self.has_up = self.z + 1 < nz
        self.has_down = self.z > 0

    def owner(self, p, x, y, z):
        return ((y * 2 + p) * self.nz + z) * 2 + x

    def greet(self):
        barrier = pltpu.get_barrier_semaphore()

        def tell(to):
            pl.semaphore_signal(barrier, inc=1, device_id=to, device_id_type=MESH)

        tell(self.other)
        tell(self.over_x)
        tell(self.over_y)
        pl.when(self.has_up)(lambda: tell(self.up))
        pl.when(self.has_down)(lambda: tell(self.down))
        peers = 3 + jnp.where(self.has_up, 1, 0) + jnp.where(self.has_down, 1, 0)
        pl.semaphore_wait(barrier, peers)


def remote(src, dst, send, recv, to):
    return pltpu.make_async_remote_copy(
        src_ref=src, dst_ref=dst, send_sem=send, recv_sem=recv, device_id=to, device_id_type=MESH
    )


def gather_kernel(
    q_in, k_in, v_in, q_all, k_all, v_all, arrive, s_up, s_down, s_x, s_y, s_two, s_near, r_near, s_own, *, nz
):
    me = Place(nz)
    half = q_all.shape[2]
    here = k_in.shape[0]
    keep = pl.ds(pl.multiple_of(me.c * half, half), half)
    give = pl.ds(pl.multiple_of((1 - me.c) * half, half), half)
    mine = pl.ds(me.c * here, here)
    own = me.owner(me.c, me.x, me.y, me.z)
    own_copies = [
        pltpu.make_async_copy(q_in.at[:, keep], q_all.at[own], s_own.at[0]),
        pltpu.make_async_copy(k_in.at[:, :, keep], k_all.at[mine], s_own.at[1]),
        pltpu.make_async_copy(v_in.at[:, :, keep], v_all.at[mine], s_own.at[2]),
    ]
    steps = 2 * nz - 2
    near = []
    for t in range(2 * here):
        src, dst = ((k_in, k_all), (v_in, v_all))[t // here]
        f = t % here
        to_slot = dst.at[me.c * here + f]
        near.append(remote(src.at[f, :, give], to_slot, s_near.at[1 + t], r_near.at[t], me.other))
    own_copies[0].start()
    me.greet()
    near_q = remote(q_in.at[:, give], q_all.at[own], s_near.at[0], arrive.at[own], me.other)
    near_q.start()
    own_copies[0].wait()

    def await_block(idx):
        remote(q_all.at[idx], q_all.at[idx], s_near.at[0], arrive.at[idx], me.over_x).wait_recv()

    def spread(p, i, off, zs):
        idx = me.owner(p, me.x, me.y, zs)
        blk = q_all.at[idx]
        up = remote(blk, blk, s_up.at[p, i], arrive.at[idx], me.up)
        down = remote(blk, blk, s_down.at[p, i], arrive.at[idx], me.down)
        return (
            (jnp.logical_and(off >= 0, me.has_up), up),
            (jnp.logical_and(off <= 0, me.has_down), down),
            (None, remote(blk, blk, s_x.at[p, i], arrive.at[idx], me.over_x)),
            (None, remote(blk, blk, s_y.at[p, i], arrive.at[idx], me.over_y)),
        )

    def begin(copies):
        for cond, copy in copies:
            if cond is None:
                copy.start()
            else:
                pl.when(cond)(copy.start)

    def sent(copies):
        for cond, copy in copies:
            if cond is None:
                copy.wait_send()
            else:
                pl.when(cond)(copy.wait_send)

    begin(spread(me.c, 0, jnp.int32(0), me.z))
    await_block(me.owner(1 - me.c, me.x, me.y, me.z))
    begin(spread(1 - me.c, 0, jnp.int32(0), me.z))

    def source(i):
        off = lax.div(i + 1, 2) * (2 * lax.rem(i, 2) - 1)
        zs = me.z - off
        return off, zs, jnp.logical_and(zs >= 0, zs < nz)

    def second(i, zs):
        a = me.owner(0, 1 - me.x, me.y, zs)
        b = me.owner(1, me.x, 1 - me.y, zs)
        return (
            (a, remote(q_all.at[a], q_all.at[a], s_two.at[0, i], arrive.at[a], me.over_y)),
            (b, remote(q_all.at[b], q_all.at[b], s_two.at[1, i], arrive.at[b], me.over_x)),
        )

    def do_second(i):
        off, zs, ok = source(i)

        @pl.when(ok)
        def _():
            for idx, copy in second(i, zs):
                await_block(idx)
                copy.start()

    def step(i, carry):
        off, zs, ok = source(i)

        @pl.when(ok)
        def _():
            for p in (0, 1):
                await_block(me.owner(p, me.x, me.y, zs))
                begin(spread(p, i, off, zs))

        do_second(i - 1)
        for t in range(2 * here):
            pl.when(i == 1 + t * steps // (2 * here))(near[t].start)
        return carry

    count = 2 * nz - 1
    lax.fori_loop(1, count, step, 0)
    do_second(jnp.int32(count - 1))
    own_copies[1].start()
    own_copies[2].start()

    def finish(i, carry):
        off, zs, ok = source(i)

        @pl.when(ok)
        def _():
            await_block(me.owner(0, me.x, 1 - me.y, zs))
            await_block(me.owner(1, 1 - me.x, me.y, zs))
            await_block(me.owner(0, 1 - me.x, 1 - me.y, zs))
            await_block(me.owner(1, 1 - me.x, 1 - me.y, zs))
            for p in (0, 1):
                sent(spread(p, i, off, zs))
            for _, copy in second(i, zs):
                copy.wait_send()

        return carry

    lax.fori_loop(0, count, finish, 0)
    near_q.wait_send()
    for copy in near:
        copy.wait()
    own_copies[1].wait()
    own_copies[2].wait()


def gather(q, k, v, devices):
    rows, width = q.shape
    frames, tok, _ = k.shape
    nz = devices // 8
    half = width // 2
    count = 2 * nz - 1
    dma = pltpu.SemaphoreType.DMA
    anywhere = pl.BlockSpec(memory_space=pl.ANY)
    vmem = pl.BlockSpec(memory_space=pltpu.VMEM)
    return pl.pallas_call(
        functools.partial(gather_kernel, nz=nz),
        out_shape=(
            jax.ShapeDtypeStruct((devices, rows, half), q.dtype),
            jax.ShapeDtypeStruct((2 * frames, tok, half), k.dtype),
            jax.ShapeDtypeStruct((2 * frames, tok, half), v.dtype),
        ),
        in_specs=[vmem, anywhere, anywhere],
        out_specs=(vmem, anywhere, anywhere),
        scratch_shapes=[
            dma((devices,)),
            dma((2, count)),
            dma((2, count)),
            dma((2, count)),
            dma((2, count)),
            dma((2, count)),
            dma((1 + 2 * frames,)),
            dma((2 * frames,)),
            dma((3,)),
        ],
        compiler_params=pltpu.CompilerParams(
            collective_id=0, has_side_effects=True, vmem_limit_bytes=VMEM_LIMIT
        ),
        name="gather",
    )(q, k, v)


def expander(heads, first, width):
    r = lax.broadcasted_iota(jnp.int32, (STAT, width), 0)
    col = lax.broadcasted_iota(jnp.int32, (STAT, width), 1)
    head = jnp.where(col < heads * HD, lax.div(col, HD), col - heads * HD - heads)
    head = jnp.where(head < 0, -STAT, jnp.where(head < heads, head, -STAT))
    return jnp.where(head + first == r, 1.0, 0.0).astype(jnp.bfloat16)


def scatter_kernel(
    msg, out, r_one, r_two, r_up, r_down, b_two, b_z, kept, att, exp_ref, exp_tot,
    sem_one, sem_two, sem_up, sem_down, s_one, s_two, s_z, sem_last, *, nz, heads
):
    me = Place(nz)
    width = heads * HD
    rows = msg.shape[1]
    count = 2 * nz - 1
    exp_ref[...] = expander(heads, 0, width + STAT)
    exp_tot[...] = expander(heads, heads, width)
    me.greet()
    lane = lax.broadcasted_iota(jnp.int32, (rows, STAT), 1)

    def target(i):
        off = lax.div(count - i, 2) * (1 - 2 * lax.rem(i, 2))
        zd = me.z + off
        return off, zd, jnp.logical_and(zd >= 0, zd < nz)

    def merge(parts):
        parts = [part.astype(jnp.float32) for part in parts]
        stats = [part[:, width:] for part in parts]
        top = functools.reduce(jnp.maximum, stats)
        total = None
        for part, st in zip(parts, stats):
            factor = jnp.exp2(st - top).astype(jnp.bfloat16)
            wide = jnp.dot(factor, exp_ref[...], preferred_element_type=jnp.float32)
            total = part * wide if total is None else total + part * wide
        tail = jnp.where(lane < heads, top, total[:, width:])
        return jnp.concatenate([total[:, :width], tail], axis=1)

    def ones(i, zd):
        a0 = me.owner(0, 1 - me.x, 1 - me.y, zd)
        a1 = me.owner(0, me.x, 1 - me.y, zd)
        b0 = me.owner(1, 1 - me.x, 1 - me.y, zd)
        b1 = me.owner(1, 1 - me.x, me.y, zd)
        return tuple(
            remote(msg.at[src], r_one.at[p, k, zd], s_one.at[p, k, zd], sem_one.at[p, k, zd], to)
            for p, k, src, to in (
                (0, 0, a0, me.over_y), (1, 0, b0, me.over_x), (0, 1, a1, me.over_y), (1, 1, b1, me.over_x)
            )
        )

    def first(i, carry):
        off, zd, ok = target(i)

        @pl.when(ok)
        def _():
            for copy in ones(i, zd):
                copy.start()

        return carry

    lax.fori_loop(0, count, first, 0)

    def twos(zd):
        return tuple(
            remote(b_two.at[p, zd], r_two.at[p, zd], s_two.at[p, zd], sem_two.at[p, zd], to)
            for p, to in ((0, me.over_x), (1, me.over_y))
        )

    def second(i):
        off, zd, ok = target(i)

        @pl.when(ok)
        def _():
            waits = ones(i, zd)
            copies = twos(zd)
            for p in (0, 1):
                waits[p].wait_recv()
                src = me.owner(0, 1 - me.x, me.y, zd) if p == 0 else me.owner(1, me.x, 1 - me.y, zd)
                b_two[p, zd] = merge([msg[src], r_one[p, 0, zd]]).astype(jnp.bfloat16)
                copies[p].start()

    def z_copies(p, zd):
        return (
            remote(b_z.at[p, zd], r_up.at[p, zd], s_z.at[p, zd], sem_up.at[p, zd], me.up),
            remote(b_z.at[p, zd], r_down.at[p, zd], s_z.at[p, zd], sem_down.at[p, zd], me.down),
        )

    def third(i):
        off, zd, ok = target(i)

        @pl.when(ok)
        def _():
            waits = ones(i, zd)
            two = twos(zd)
            for p in (0, 1):
                up, down = z_copies(p, zd)
                waits[2 + p].wait_recv()
                two[p].wait_recv()
                here = merge([msg[me.owner(p, me.x, me.y, zd)], r_one[p, 1, zd], r_two[p, zd]])
                kept[p] = here

                @pl.when(jnp.logical_and(off >= 0, me.has_down))
                def _():
                    up.wait_recv()
                    kept[p] = merge([kept[p], r_up[p, zd]])

                @pl.when(jnp.logical_and(off <= 0, me.has_up))
                def _():
                    down.wait_recv()
                    kept[p] = merge([kept[p], r_down[p, zd]])

                @pl.when(off != 0)
                def _():
                    b_z[p, zd] = kept[p].astype(jnp.bfloat16)

                pl.when(off > 0)(up.start)
                pl.when(off < 0)(down.start)

    def step(i, carry):
        second(i)
        pl.when(i > 0)(lambda: third(i - 1))
        return carry

    lax.fori_loop(0, count, step, 0)
    third(jnp.int32(count - 1))

    for p in (0, 1):
        full = kept[p]
        tail = full[:, width:]
        inverse = 1.0 / jnp.where(jnp.logical_and(lane >= heads, lane < 2 * heads), tail, 1.0)
        hi = inverse.astype(jnp.bfloat16)
        lo = (inverse - hi.astype(jnp.float32)).astype(jnp.bfloat16)
        wide = jnp.dot(hi, exp_tot[...], preferred_element_type=jnp.float32)
        wide = wide + jnp.dot(lo, exp_tot[...], preferred_element_type=jnp.float32)
        att[p] = (full[:, :width] * wide).astype(jnp.bfloat16)
    last = remote(att.at[1 - me.c], out.at[me.c], sem_last.at[0], sem_last.at[1], me.other)
    last.start()
    out[me.c] = att[me.c]

    def finish(i, carry):
        off, zd, ok = target(i)

        @pl.when(ok)
        def _():
            for copy in ones(i, zd):
                copy.wait_send()
            for copy in twos(zd):
                copy.wait_send()
            for p in (0, 1):
                up, down = z_copies(p, zd)
                pl.when(off > 0)(up.wait_send)
                pl.when(off < 0)(down.wait_send)

        return carry

    lax.fori_loop(0, count, finish, 0)
    last.wait()


def scatter(msg, heads):
    devices, rows, wide = msg.shape
    nz = devices // 8
    width = heads * HD
    dma = pltpu.SemaphoreType.DMA
    vmem = pl.BlockSpec(memory_space=pltpu.VMEM)
    block = (rows, wide)
    return pl.pallas_call(
        functools.partial(scatter_kernel, nz=nz, heads=heads),
        out_shape=jax.ShapeDtypeStruct((2, rows, width), jnp.bfloat16),
        in_specs=[vmem],
        out_specs=vmem,
        scratch_shapes=[
            pltpu.VMEM((2, 2, nz) + block, jnp.bfloat16),
            pltpu.VMEM((2, nz) + block, jnp.bfloat16),
            pltpu.VMEM((2, nz) + block, jnp.bfloat16),
            pltpu.VMEM((2, nz) + block, jnp.bfloat16),
            pltpu.VMEM((2, nz) + block, jnp.bfloat16),
            pltpu.VMEM((2, nz) + block, jnp.bfloat16),
            pltpu.VMEM((2,) + block, jnp.float32),
            pltpu.VMEM((2, rows, width), jnp.bfloat16),
            pltpu.VMEM((STAT, wide), jnp.bfloat16),
            pltpu.VMEM((STAT, width), jnp.bfloat16),
            dma((2, 2, nz)),
            dma((2, nz)),
            dma((2, nz)),
            dma((2, nz)),
            dma((2, 2, nz)),
            dma((2, nz)),
            dma((2, nz)),
            dma((2,)),
        ],
        compiler_params=pltpu.CompilerParams(
            collective_id=1, has_side_effects=True, vmem_limit_bytes=VMEM_LIMIT
        ),
        name="scatter",
    )(msg)


def needed_frames(rows, frame_slot, covisible, counts):
    frame_ids = jnp.arange(frame_slot.shape[0], dtype=jnp.int32)
    hits = frame_slot[None, :] == rows[:, None]
    frames = jnp.sum(jnp.where(hits, frame_ids[None, :], 0), axis=1)
    in_list = jnp.arange(covisible.shape[1], dtype=jnp.int32)[None, :] < counts[:, None]
    match = (covisible[:, :, None] == frames[None, None, :]) & in_list[:, :, None]
    return jnp.any(match, axis=1).astype(jnp.int32)


def body_cores(devices, per_group, queries, keys, values, frame_slot, covisible, counts, out_weight):
    here, tok, width = keys.shape
    heads = width // HD // 2
    g, d = lax.axis_index("group"), lax.axis_index("dev")
    base = (lax.div(g, 2) * 2 * per_group + d) * here
    rows = jnp.arange(here, dtype=jnp.int32) + base
    rows = jnp.concatenate([rows, rows + per_group * here])
    flags = needed_frames(rows, frame_slot, covisible, counts).reshape(-1)
    q_all, k_all, v_all = gather(queries, keys, values, devices)
    own = queries.shape[0]
    msg = attend(flags, q_all.reshape(devices * own, width // 2), k_all, v_all)
    halves = scatter(msg.reshape(devices, own, -1), heads)
    weight = out_weight.reshape(2, width // 2, -1)
    return jnp.einsum("hrd,hde->re", halves, weight, preferred_element_type=jnp.float32).astype(jnp.bfloat16)


def body_any(queries, keys, values, frame_slot, covisible, counts, out_weight):
    axes = ("group", "dev")
    here, tok, width = keys.shape
    heads = width // HD
    rows = jnp.arange(here, dtype=jnp.int32) + lax.axis_index(axes) * here
    flags = needed_frames(rows, frame_slot, covisible, counts).reshape(-1)
    q_all = lax.all_gather(queries, axes, axis=0, tiled=True)
    msg = attend(flags, q_all, keys, values).astype(jnp.float32)
    top = msg[:, width : width + heads]
    totals = msg[:, width + heads : width + 2 * heads]
    factor = jnp.exp2(top - lax.pmax(top, axes))
    numer = msg[:, :width] * jnp.repeat(factor, HD, axis=1)
    own_numer = lax.psum_scatter(numer, axes, scatter_dimension=0, tiled=True)
    own_totals = lax.psum_scatter(totals * factor, axes, scatter_dimension=0, tiled=True)
    attended = (own_numer / jnp.repeat(own_totals, HD, axis=1)).astype(jnp.bfloat16)
    return jnp.dot(attended, out_weight, preferred_element_type=jnp.float32).astype(jnp.bfloat16)


def solution(mesh):
    group, dev = mesh.shape["group"], mesh.shape["dev"]
    body = body_any
    if group == 4 and dev % 2 == 0:
        body = functools.partial(body_cores, group * dev, dev)
    return jax.shard_map(
        body,
        mesh=mesh,
        in_specs=(
            P(("group", "dev"), None),
            P(("group", "dev"), None, None),
            P(("group", "dev"), None, None),
            P(),
            P(),
            P(),
            P(),
        ),
        out_specs=P(("group", "dev"), None),
        check_vma=False,
    )
```

```python
import functools

import jax
import jax.numpy as jnp
from jax import lax
from jax.experimental import pallas as pl
from jax.experimental.pallas import tpu as pltpu
from jax.sharding import PartitionSpec as P

HD = 64
NEG_FILL = -1e30
LOG2E = 1.4426950408889634
MESH = pl.DeviceIdType.MESH
STAT = 128
TOP_STEP = 8.0
SMALL = 60.0
VMEM_LIMIT = 56 * 1024 * 1024


def attend_kernel(flags, q_ref, k_ref, v_ref, out_ref, vt, qt, acc, stat, *, heads, frames, tok, qframes):
    width = heads * HD
    scale = LOG2E * HD ** (-0.5)

    row_id = lax.broadcasted_iota(jnp.int32, (width, 128), 0)
    col_id = lax.broadcasted_iota(jnp.int32, (width, 128), 1)
    by_head = jnp.where(lax.div(row_id, HD) == col_id, 1.0, 0.0).astype(jnp.bfloat16)

    def largest_square(block):
        squares = jnp.dot(block * block, by_head, preferred_element_type=jnp.float32)
        return jnp.max(squares, axis=0, keepdims=True)

    def turn(f, largest):
        turned = v_ref[f].T
        for h in range(heads):
            vt[f, h, 0:HD, :] = turned[h * HD : (h + 1) * HD, :]
            vt[f, h, HD : HD + 16, :] = jnp.ones((16, tok), jnp.bfloat16)
        return jnp.maximum(largest, largest_square(k_ref[f]))

    key_square = lax.fori_loop(0, frames, turn, jnp.zeros((1, 128), jnp.float32))
    stat[...] = jnp.zeros_like(stat)
    qt[...] = jnp.zeros_like(qt)

    def one_query(qi, carry):
        rows = pl.ds(pl.multiple_of(qi * tok, tok), tok)
        for g in range(heads // 2):
            pair = q_ref[rows, g * 128 : (g + 1) * 128].T
            qt[2 * g, 0:HD, :] = pair[0:HD, :]
            qt[2 * g + 1, HD:128, :] = pair[HD:128, :]
        acc[...] = jnp.zeros_like(acc)
        stat[0:heads, :] = jnp.full((heads, tok), NEG_FILL, jnp.float32)
        bound = jnp.max(largest_square(q_ref[rows, :]) * key_square) * (scale * scale)
        small = bound <= SMALL * SMALL

        def scores(f, h):
            kp = k_ref[f, :, (h // 2) * 128 : (h // 2 + 1) * 128]
            return jnp.dot(kp, qt[h], preferred_element_type=jnp.float32)

        def small_frame(f):
            stat[0:heads, :] = jnp.zeros((heads, tok), jnp.float32)
            for h in range(heads):
                p = jnp.exp2(scores(f, h) * scale).astype(jnp.bfloat16)
                acc[h] += jnp.dot(vt[f, h], p, preferred_element_type=jnp.float32)

        def any_frame(f):
            for h in range(heads):
                s = scores(f, h)
                top = jnp.max(s, axis=0, keepdims=True) * scale
                old = stat[h : h + 1, :]
                new = jnp.maximum(old, jnp.ceil(top * (1.0 / TOP_STEP)) * TOP_STEP)
                p = jnp.exp2(s * scale - new).astype(jnp.bfloat16)
                add = jnp.dot(vt[f, h], p, preferred_element_type=jnp.float32)
                acc[h] = acc[h] * jnp.exp2(old - new) + add
                stat[h : h + 1, :] = new

        def one_frame(f, c):
            needed = flags[qi * frames + f] != 0
            pl.when(jnp.logical_and(needed, small))(lambda: small_frame(f))
            pl.when(jnp.logical_and(needed, jnp.logical_not(small)))(lambda: any_frame(f))
            return c

        lax.fori_loop(0, frames, one_frame, 0)
        for h in range(heads):
            stat[heads + h : heads + h + 1, :] = acc[h, HD : HD + 1, :]
        for g in range(heads // 2):
            both = jnp.concatenate([acc[2 * g, 0:HD, :], acc[2 * g + 1, 0:HD, :]], axis=0)
            out_ref[rows, g * 128 : (g + 1) * 128] = both.astype(jnp.bfloat16).T
        out_ref[rows, width : width + STAT] = stat[...].astype(jnp.bfloat16).T
        return carry

    lax.fori_loop(0, qframes, one_query, 0)


def attend(flags, q, k, v):
    rows, width = q.shape
    frames, tok = k.shape[0], k.shape[1]
    heads = width // HD
    qframes = rows // tok
    return pl.pallas_call(
        functools.partial(attend_kernel, heads=heads, frames=frames, tok=tok, qframes=qframes),
        out_shape=jax.ShapeDtypeStruct((rows, width + STAT), jnp.bfloat16),
        in_specs=[pl.BlockSpec(memory_space=pltpu.SMEM)] + [pl.BlockSpec(memory_space=pltpu.VMEM)] * 3,
        out_specs=pl.BlockSpec(memory_space=pltpu.VMEM),
        scratch_shapes=[
            pltpu.VMEM((frames, heads, HD + 16, tok), jnp.bfloat16),
            pltpu.VMEM((heads, 128, tok), jnp.bfloat16),
            pltpu.VMEM((heads, HD + 16, tok), jnp.float32),
            pltpu.VMEM((STAT, tok), jnp.float32),
        ],
        compiler_params=pltpu.CompilerParams(vmem_limit_bytes=VMEM_LIMIT),
        name="attend",
    )(flags, q, k, v)


class Place:
    def __init__(self, nz):
        g, d = lax.axis_index("group"), lax.axis_index("dev")
        self.nz = nz
        self.y, self.c = lax.div(g, 2), lax.rem(g, 2)
        self.z, self.x = lax.div(d, 2), lax.rem(d, 2)
        self.other = (self.y * 2 + 1 - self.c, d)
        self.over_x = (g, self.z * 2 + 1 - self.x)
        self.over_y = ((1 - self.y) * 2 + self.c, d)
        self.up = (g, (self.z + 1) * 2 + self.x)
        self.down = (g, (self.z - 1) * 2 + self.x)
        self.has_up = self.z + 1 < nz
        self.has_down = self.z > 0

    def owner(self, p, x, y, z):
        return ((y * 2 + p) * self.nz + z) * 2 + x

    def greet(self):
        barrier = pltpu.get_barrier_semaphore()

        def tell(to):
            pl.semaphore_signal(barrier, inc=1, device_id=to, device_id_type=MESH)

        tell(self.other)
        tell(self.over_x)
        tell(self.over_y)
        pl.when(self.has_up)(lambda: tell(self.up))
        pl.when(self.has_down)(lambda: tell(self.down))
        peers = 3 + jnp.where(self.has_up, 1, 0) + jnp.where(self.has_down, 1, 0)
        pl.semaphore_wait(barrier, peers)


def remote(src, dst, send, recv, to):
    return pltpu.make_async_remote_copy(
        src_ref=src, dst_ref=dst, send_sem=send, recv_sem=recv, device_id=to, device_id_type=MESH
    )


def gather_kernel(
    q_in, k_in, v_in, q_all, k_all, v_all, parcel, arrive, s_up, s_down, s_x, s_y, s_two, s_near, r_near, s_own, s_load, *, nz
):
    me = Place(nz)
    half = q_all.shape[2]
    here = k_in.shape[0]
    keep = pl.ds(pl.multiple_of(me.c * half, half), half)
    give = pl.ds(pl.multiple_of((1 - me.c) * half, half), half)
    mine = pl.ds(me.c * here, here)
    own = me.owner(me.c, me.x, me.y, me.z)
    own_copies = [
        pltpu.make_async_copy(q_in.at[:, keep], q_all.at[own], s_own.at[0]),
        pltpu.make_async_copy(k_in.at[:, :, keep], k_all.at[mine], s_own.at[1]),
        pltpu.make_async_copy(v_in.at[:, :, keep], v_all.at[mine], s_own.at[2]),
    ]
    steps = 2 * nz - 2
    near = []
    for t in range(2 * here):
        to_slot = (k_all, v_all)[t // here].at[me.c * here + t % here]
        near.append(remote(parcel.at[t], to_slot, s_near.at[1 + t], r_near.at[t], me.other))
    own_copies[0].start()
    loads = []
    for t in range(2 * here):
        src = (k_in, v_in)[t // here]
        loads.append(pltpu.make_async_copy(src.at[t % here, :, give], parcel.at[t], s_load.at[t]))
        loads[t].start()
    own_copies[1].start()
    own_copies[2].start()
    me.greet()
    near_q = remote(q_in.at[:, give], q_all.at[own], s_near.at[0], arrive.at[own], me.other)
    near_q.start()
    own_copies[0].wait()

    def await_block(idx):
        remote(q_all.at[idx], q_all.at[idx], s_near.at[0], arrive.at[idx], me.over_x).wait_recv()

    def spread(p, i, off, zs):
        idx = me.owner(p, me.x, me.y, zs)
        blk = q_all.at[idx]
        up = remote(blk, blk, s_up.at[p, i], arrive.at[idx], me.up)
        down = remote(blk, blk, s_down.at[p, i], arrive.at[idx], me.down)
        return (
            (jnp.logical_and(off >= 0, me.has_up), up),
            (jnp.logical_and(off <= 0, me.has_down), down),
            (None, remote(blk, blk, s_x.at[p, i], arrive.at[idx], me.over_x)),
            (None, remote(blk, blk, s_y.at[p, i], arrive.at[idx], me.over_y)),
        )

    def begin(copies):
        for cond, copy in copies:
            if cond is None:
                copy.start()
            else:
                pl.when(cond)(copy.start)

    def sent(copies):
        for cond, copy in copies:
            if cond is None:
                copy.wait_send()
            else:
                pl.when(cond)(copy.wait_send)

    begin(spread(me.c, 0, jnp.int32(0), me.z))
    await_block(me.owner(1 - me.c, me.x, me.y, me.z))
    begin(spread(1 - me.c, 0, jnp.int32(0), me.z))

    def source(i):
        off = lax.div(i + 1, 2) * (2 * lax.rem(i, 2) - 1)
        zs = me.z - off
        return off, zs, jnp.logical_and(zs >= 0, zs < nz)

    def second(i, zs):
        a = me.owner(0, 1 - me.x, me.y, zs)
        b = me.owner(1, me.x, 1 - me.y, zs)
        return (
            (a, remote(q_all.at[a], q_all.at[a], s_two.at[0, i], arrive.at[a], me.over_y)),
            (b, remote(q_all.at[b], q_all.at[b], s_two.at[1, i], arrive.at[b], me.over_x)),
        )

    def do_second(i):
        off, zs, ok = source(i)

        @pl.when(ok)
        def _():
            for idx, copy in second(i, zs):
                await_block(idx)
                copy.start()

    def step(i, carry):
        off, zs, ok = source(i)

        @pl.when(ok)
        def _():
            for p in (0, 1):
                await_block(me.owner(p, me.x, me.y, zs))
                begin(spread(p, i, off, zs))

        do_second(i - 1)
        for t in range(2 * here):

            @pl.when(i == 1 + t * steps // (2 * here))
            def _():
                loads[t].wait()
                near[t].start()

        return carry

    count = 2 * nz - 1
    lax.fori_loop(1, count, step, 0)
    do_second(jnp.int32(count - 1))

    def finish(i, carry):
        off, zs, ok = source(i)

        @pl.when(ok)
        def _():
            await_block(me.owner(0, me.x, 1 - me.y, zs))
            await_block(me.owner(1, 1 - me.x, me.y, zs))
            await_block(me.owner(0, 1 - me.x, 1 - me.y, zs))
            await_block(me.owner(1, 1 - me.x, 1 - me.y, zs))
            for p in (0, 1):
                sent(spread(p, i, off, zs))
            for _, copy in second(i, zs):
                copy.wait_send()

        return carry

    lax.fori_loop(0, count, finish, 0)
    near_q.wait_send()
    for copy in near:
        copy.wait()
    own_copies[1].wait()
    own_copies[2].wait()


def gather(q, k, v, devices):
    rows, width = q.shape
    frames, tok, _ = k.shape
    nz = devices // 8
    half = width // 2
    count = 2 * nz - 1
    dma = pltpu.SemaphoreType.DMA
    anywhere = pl.BlockSpec(memory_space=pl.ANY)
    vmem = pl.BlockSpec(memory_space=pltpu.VMEM)
    return pl.pallas_call(
        functools.partial(gather_kernel, nz=nz),
        out_shape=(
            jax.ShapeDtypeStruct((devices, rows, half), q.dtype),
            jax.ShapeDtypeStruct((2 * frames, tok, half), k.dtype),
            jax.ShapeDtypeStruct((2 * frames, tok, half), v.dtype),
        ),
        in_specs=[vmem, anywhere, anywhere],
        out_specs=(vmem,) * 3,
        scratch_shapes=[
            pltpu.VMEM((2 * frames, tok, half), k.dtype),
            dma((devices,)),
            dma((2, count)),
            dma((2, count)),
            dma((2, count)),
            dma((2, count)),
            dma((2, count)),
            dma((1 + 2 * frames,)),
            dma((2 * frames,)),
            dma((3,)),
            dma((2 * frames,)),
        ],
        compiler_params=pltpu.CompilerParams(
            collective_id=0, has_side_effects=True, vmem_limit_bytes=VMEM_LIMIT
        ),
        name="gather",
    )(q, k, v)


def expander(heads, first, width):
    r = lax.broadcasted_iota(jnp.int32, (STAT, width), 0)
    col = lax.broadcasted_iota(jnp.int32, (STAT, width), 1)
    head = jnp.where(col < heads * HD, lax.div(col, HD), col - heads * HD - heads)
    head = jnp.where(head < 0, -STAT, jnp.where(head < heads, head, -STAT))
    return jnp.where(head + first == r, 1.0, 0.0).astype(jnp.bfloat16)


def scatter_kernel(
    msg, out, r_one, r_two, r_up, r_down, b_two, b_z, kept, att, exp_ref, exp_tot,
    sem_one, sem_two, sem_up, sem_down, s_one, s_two, s_z, sem_last, *, nz, heads
):
    me = Place(nz)
    width = heads * HD
    rows = msg.shape[1]
    count = 2 * nz - 1
    exp_ref[...] = expander(heads, 0, width + STAT)
    exp_tot[...] = expander(heads, heads, width)
    me.greet()
    lane = lax.broadcasted_iota(jnp.int32, (rows, STAT), 1)

    def target(i):
        off = lax.div(count - i, 2) * (1 - 2 * lax.rem(i, 2))
        zd = me.z + off
        return off, zd, jnp.logical_and(zd >= 0, zd < nz)

    def merge(parts):
        parts = [part.astype(jnp.float32) for part in parts]
        stats = [part[:, width:] for part in parts]
        top = functools.reduce(jnp.maximum, stats)
        total = None
        for part, st in zip(parts, stats):
            factor = jnp.exp2(st - top).astype(jnp.bfloat16)
            wide = jnp.dot(factor, exp_ref[...], preferred_element_type=jnp.float32)
            total = part * wide if total is None else total + part * wide
        tail = jnp.where(lane < heads, top, total[:, width:])
        return jnp.concatenate([total[:, :width], tail], axis=1)

    def ones(i, zd):
        a0 = me.owner(0, 1 - me.x, 1 - me.y, zd)
        a1 = me.owner(0, me.x, 1 - me.y, zd)
        b0 = me.owner(1, 1 - me.x, 1 - me.y, zd)
        b1 = me.owner(1, 1 - me.x, me.y, zd)
        return tuple(
            remote(msg.at[src], r_one.at[p, k, zd], s_one.at[p, k, zd], sem_one.at[p, k, zd], to)
            for p, k, src, to in (
                (0, 0, a0, me.over_y), (1, 0, b0, me.over_x), (0, 1, a1, me.over_y), (1, 1, b1, me.over_x)
            )
        )

    def first(i, carry):
        off, zd, ok = target(i)

        @pl.when(ok)
        def _():
            for copy in ones(i, zd):
                copy.start()

        return carry

    lax.fori_loop(0, count, first, 0)

    def twos(zd):
        return tuple(
            remote(b_two.at[p, zd], r_two.at[p, zd], s_two.at[p, zd], sem_two.at[p, zd], to)
            for p, to in ((0, me.over_x), (1, me.over_y))
        )

    def second(i):
        off, zd, ok = target(i)

        @pl.when(ok)
        def _():
            waits = ones(i, zd)
            copies = twos(zd)
            for p in (0, 1):
                waits[p].wait_recv()
                src = me.owner(0, 1 - me.x, me.y, zd) if p == 0 else me.owner(1, me.x, 1 - me.y, zd)
                b_two[p, zd] = merge([msg[src], r_one[p, 0, zd]]).astype(jnp.bfloat16)
                copies[p].start()

    def z_copies(p, zd):
        return (
            remote(b_z.at[p, zd], r_up.at[p, zd], s_z.at[p, zd], sem_up.at[p, zd], me.up),
            remote(b_z.at[p, zd], r_down.at[p, zd], s_z.at[p, zd], sem_down.at[p, zd], me.down),
        )

    def third(i):
        off, zd, ok = target(i)

        @pl.when(ok)
        def _():
            waits = ones(i, zd)
            two = twos(zd)
            for p in (0, 1):
                up, down = z_copies(p, zd)
                waits[2 + p].wait_recv()
                two[p].wait_recv()
                here = merge([msg[me.owner(p, me.x, me.y, zd)], r_one[p, 1, zd], r_two[p, zd]])
                kept[p] = here

                @pl.when(jnp.logical_and(off >= 0, me.has_down))
                def _():
                    up.wait_recv()
                    kept[p] = merge([kept[p], r_up[p, zd]])

                @pl.when(jnp.logical_and(off <= 0, me.has_up))
                def _():
                    down.wait_recv()
                    kept[p] = merge([kept[p], r_down[p, zd]])

                @pl.when(off != 0)
                def _():
                    b_z[p, zd] = kept[p].astype(jnp.bfloat16)

                pl.when(off > 0)(up.start)
                pl.when(off < 0)(down.start)

    def step(i, carry):
        second(i)
        pl.when(i > 0)(lambda: third(i - 1))
        return carry

    lax.fori_loop(0, count, step, 0)
    third(jnp.int32(count - 1))

    for p in (0, 1):
        full = kept[p]
        tail = full[:, width:]
        inverse = 1.0 / jnp.where(jnp.logical_and(lane >= heads, lane < 2 * heads), tail, 1.0)
        hi = inverse.astype(jnp.bfloat16)
        lo = (inverse - hi.astype(jnp.float32)).astype(jnp.bfloat16)
        wide = jnp.dot(hi, exp_tot[...], preferred_element_type=jnp.float32)
        wide = wide + jnp.dot(lo, exp_tot[...], preferred_element_type=jnp.float32)
        att[p] = (full[:, :width] * wide).astype(jnp.bfloat16)
    last = remote(att.at[1 - me.c], out.at[me.c], sem_last.at[0], sem_last.at[1], me.other)
    last.start()
    out[me.c] = att[me.c]

    def finish(i, carry):
        off, zd, ok = target(i)

        @pl.when(ok)
        def _():
            for copy in ones(i, zd):
                copy.wait_send()
            for copy in twos(zd):
                copy.wait_send()
            for p in (0, 1):
                up, down = z_copies(p, zd)
                pl.when(off > 0)(up.wait_send)
                pl.when(off < 0)(down.wait_send)

        return carry

    lax.fori_loop(0, count, finish, 0)
    last.wait()


def scatter(msg, heads):
    devices, rows, wide = msg.shape
    nz = devices // 8
    width = heads * HD
    dma = pltpu.SemaphoreType.DMA
    vmem = pl.BlockSpec(memory_space=pltpu.VMEM)
    block = (rows, wide)
    return pl.pallas_call(
        functools.partial(scatter_kernel, nz=nz, heads=heads),
        out_shape=jax.ShapeDtypeStruct((2, rows, width), jnp.bfloat16),
        in_specs=[vmem],
        out_specs=vmem,
        scratch_shapes=[
            pltpu.VMEM((2, 2, nz) + block, jnp.bfloat16),
            pltpu.VMEM((2, nz) + block, jnp.bfloat16),
            pltpu.VMEM((2, nz) + block, jnp.bfloat16),
            pltpu.VMEM((2, nz) + block, jnp.bfloat16),
            pltpu.VMEM((2, nz) + block, jnp.bfloat16),
            pltpu.VMEM((2, nz) + block, jnp.bfloat16),
            pltpu.VMEM((2,) + block, jnp.float32),
            pltpu.VMEM((2, rows, width), jnp.bfloat16),
            pltpu.VMEM((STAT, wide), jnp.bfloat16),
            pltpu.VMEM((STAT, width), jnp.bfloat16),
            dma((2, 2, nz)),
            dma((2, nz)),
            dma((2, nz)),
            dma((2, nz)),
            dma((2, 2, nz)),
            dma((2, nz)),
            dma((2, nz)),
            dma((2,)),
        ],
        compiler_params=pltpu.CompilerParams(
            collective_id=1, has_side_effects=True, vmem_limit_bytes=VMEM_LIMIT
        ),
        name="scatter",
    )(msg)


def needed_frames(rows, frame_slot, covisible, counts):
    frame_ids = jnp.arange(frame_slot.shape[0], dtype=jnp.int32)
    hits = frame_slot[None, :] == rows[:, None]
    frames = jnp.sum(jnp.where(hits, frame_ids[None, :], 0), axis=1)
    in_list = jnp.arange(covisible.shape[1], dtype=jnp.int32)[None, :] < counts[:, None]
    match = (covisible[:, :, None] == frames[None, None, :]) & in_list[:, :, None]
    return jnp.any(match, axis=1).astype(jnp.int32)


def body_cores(devices, per_group, queries, keys, values, frame_slot, covisible, counts, out_weight):
    here, tok, width = keys.shape
    heads = width // HD // 2
    g, d = lax.axis_index("group"), lax.axis_index("dev")
    base = (lax.div(g, 2) * 2 * per_group + d) * here
    rows = jnp.arange(here, dtype=jnp.int32) + base
    rows = jnp.concatenate([rows, rows + per_group * here])
    flags = needed_frames(rows, frame_slot, covisible, counts).reshape(-1)
    q_all, k_all, v_all = gather(queries, keys, values, devices)
    own = queries.shape[0]
    msg = attend(flags, q_all.reshape(devices * own, width // 2), k_all, v_all)
    halves = scatter(msg.reshape(devices, own, -1), heads)
    weight = out_weight.reshape(2, width // 2, -1)
    return jnp.einsum("hrd,hde->re", halves, weight, preferred_element_type=jnp.float32).astype(jnp.bfloat16)


def body_any(queries, keys, values, frame_slot, covisible, counts, out_weight):
    axes = ("group", "dev")
    here, tok, width = keys.shape
    heads = width // HD
    rows = jnp.arange(here, dtype=jnp.int32) + lax.axis_index(axes) * here
    flags = needed_frames(rows, frame_slot, covisible, counts).reshape(-1)
    q_all = lax.all_gather(queries, axes, axis=0, tiled=True)
    msg = attend(flags, q_all, keys, values).astype(jnp.float32)
    top = msg[:, width : width + heads]
    totals = msg[:, width + heads : width + 2 * heads]
    factor = jnp.exp2(top - lax.pmax(top, axes))
    numer = msg[:, :width] * jnp.repeat(factor, HD, axis=1)
    own_numer = lax.psum_scatter(numer, axes, scatter_dimension=0, tiled=True)
    own_totals = lax.psum_scatter(totals * factor, axes, scatter_dimension=0, tiled=True)
    attended = (own_numer / jnp.repeat(own_totals, HD, axis=1)).astype(jnp.bfloat16)
    return jnp.dot(attended, out_weight, preferred_element_type=jnp.float32).astype(jnp.bfloat16)


def solution(mesh):
    group, dev = mesh.shape["group"], mesh.shape["dev"]
    body = body_any
    if group == 4 and dev % 2 == 0:
        body = functools.partial(body_cores, group * dev, dev)
    return jax.shard_map(
        body,
        mesh=mesh,
        in_specs=(
            P(("group", "dev"), None),
            P(("group", "dev"), None, None),
            P(("group", "dev"), None, None),
            P(),
            P(),
            P(),
            P(),
        ),
        out_specs=P(("group", "dev"), None),
        check_vma=False,
    )
```

```python
import functools

import jax
import jax.numpy as jnp
from jax import lax
from jax.experimental import pallas as pl
from jax.experimental.pallas import tpu as pltpu
from jax.sharding import PartitionSpec as P

HD = 64
NEG_FILL = -1e30
LOG2E = 1.4426950408889634
MESH = pl.DeviceIdType.MESH
STAT = 128
TOP_STEP = 8.0
SMALL = 60.0
VMEM_LIMIT = 56 * 1024 * 1024


def head_lanes(width):
    row_id = lax.broadcasted_iota(jnp.int32, (width, 128), 0)
    col_id = lax.broadcasted_iota(jnp.int32, (width, 128), 1)
    return jnp.where(lax.div(row_id, HD) == col_id, 1.0, 0.0).astype(jnp.bfloat16)


def largest_square(block, by_head):
    squares = jnp.dot(block * block, by_head, preferred_element_type=jnp.float32)
    return jnp.max(squares, axis=0, keepdims=True)


def turn_values(block, put, heads):
    turned = block.T
    for h in range(heads):
        put(h, slice(0, HD), turned[h * HD : (h + 1) * HD, :])
        put(h, slice(HD, HD + 16), jnp.ones((16, block.shape[0]), block.dtype))


def attend_kernel(flags, q_ref, k_ref, vt, ks_ref, out_ref, qt, acc, stat, *, heads, frames, tok, qframes):
    width = heads * HD
    scale = LOG2E * HD ** (-0.5)

    by_head = head_lanes(width)
    key_square = ks_ref[0:1, :]
    stat[...] = jnp.zeros_like(stat)
    qt[...] = jnp.zeros_like(qt)

    def one_query(qi, carry):
        rows = pl.ds(pl.multiple_of(qi * tok, tok), tok)
        for g in range(heads // 2):
            pair = q_ref[rows, g * 128 : (g + 1) * 128].T
            qt[2 * g, 0:HD, :] = pair[0:HD, :]
            qt[2 * g + 1, HD:128, :] = pair[HD:128, :]
        acc[...] = jnp.zeros_like(acc)
        stat[0:heads, :] = jnp.full((heads, tok), NEG_FILL, jnp.float32)
        bound = jnp.max(largest_square(q_ref[rows, :], by_head) * key_square) * (scale * scale)
        small = bound <= SMALL * SMALL

        def scores(f, h):
            kp = k_ref[f, :, (h // 2) * 128 : (h // 2 + 1) * 128]
            return jnp.dot(kp, qt[h], preferred_element_type=jnp.float32)

        def small_frame(f):
            stat[0:heads, :] = jnp.zeros((heads, tok), jnp.float32)

            def weigh(s):
                return jnp.exp2(s * scale).astype(jnp.bfloat16)

            def add(h, p):
                acc[h] += jnp.dot(vt[f, h], p, preferred_element_type=jnp.float32)

            s, p = scores(f, 0), None
            for h in range(heads):
                later = scores(f, h + 1) if h + 1 < heads else None
                now = weigh(s)
                if h > 0:
                    add(h - 1, p)
                s, p = later, now
            add(heads - 1, p)

        def any_frame(f):
            for h in range(heads):
                s = scores(f, h)
                top = jnp.max(s, axis=0, keepdims=True) * scale
                old = stat[h : h + 1, :]
                new = jnp.maximum(old, jnp.ceil(top * (1.0 / TOP_STEP)) * TOP_STEP)
                p = jnp.exp2(s * scale - new).astype(jnp.bfloat16)
                add = jnp.dot(vt[f, h], p, preferred_element_type=jnp.float32)
                acc[h] = acc[h] * jnp.exp2(old - new) + add
                stat[h : h + 1, :] = new

        def one_frame(f, c):
            needed = flags[qi, f] != 0
            pl.when(jnp.logical_and(needed, small))(lambda: small_frame(f))
            pl.when(jnp.logical_and(needed, jnp.logical_not(small)))(lambda: any_frame(f))
            return c

        lax.fori_loop(0, frames, one_frame, 0)
        for h in range(heads):
            stat[heads + h : heads + h + 1, :] = acc[h, HD : HD + 1, :]
        for g in range(heads // 2):
            both = jnp.concatenate([acc[2 * g, 0:HD, :], acc[2 * g + 1, 0:HD, :]], axis=0)
            out_ref[rows, g * 128 : (g + 1) * 128] = both.astype(jnp.bfloat16).T
        out_ref[rows, width : width + STAT] = stat[...].astype(jnp.bfloat16).T
        return carry

    lax.fori_loop(0, qframes, one_query, 0)


def attend(flags, q, k, vt, key_square):
    rows, width = q.shape
    frames, tok = k.shape[0], k.shape[1]
    heads = width // HD
    qframes = rows // tok
    return pl.pallas_call(
        functools.partial(attend_kernel, heads=heads, frames=frames, tok=tok, qframes=qframes),
        out_shape=jax.ShapeDtypeStruct((rows, width + STAT), jnp.bfloat16),
        in_specs=[pl.BlockSpec(memory_space=pltpu.SMEM)] + [pl.BlockSpec(memory_space=pltpu.VMEM)] * 4,
        out_specs=pl.BlockSpec(memory_space=pltpu.VMEM),
        scratch_shapes=[
            pltpu.VMEM((heads, 128, tok), jnp.bfloat16),
            pltpu.VMEM((heads, HD + 16, tok), jnp.float32),
            pltpu.VMEM((STAT, tok), jnp.float32),
        ],
        compiler_params=pltpu.CompilerParams(vmem_limit_bytes=VMEM_LIMIT),
        name="attend",
    )(flags, q, k, vt, key_square)


def prepare_kernel(k_ref, v_ref, vt, ks_ref, *, heads, frames):
    by_head = head_lanes(k_ref.shape[2])

    def one(f, largest):
        def put(h, part, block):
            vt[f, h, part, :] = block

        turn_values(v_ref[f], put, heads)
        return jnp.maximum(largest, largest_square(k_ref[f], by_head))

    largest = lax.fori_loop(0, frames, one, jnp.zeros((1, 128), jnp.float32))
    ks_ref[...] = jnp.broadcast_to(largest, ks_ref.shape)


def prepare(k, v):
    frames, tok, width = k.shape
    heads = width // HD
    return pl.pallas_call(
        functools.partial(prepare_kernel, heads=heads, frames=frames),
        out_shape=(
            jax.ShapeDtypeStruct((frames, heads, HD + 16, tok), v.dtype),
            jax.ShapeDtypeStruct((8, 128), jnp.float32),
        ),
        compiler_params=pltpu.CompilerParams(vmem_limit_bytes=VMEM_LIMIT),
        name="prepare",
    )(k, v)


class Place:
    def __init__(self, nz):
        g, d = lax.axis_index("group"), lax.axis_index("dev")
        self.nz = nz
        self.y, self.c = lax.div(g, 2), lax.rem(g, 2)
        self.z, self.x = lax.div(d, 2), lax.rem(d, 2)
        self.other = (self.y * 2 + 1 - self.c, d)
        self.over_x = (g, self.z * 2 + 1 - self.x)
        self.over_y = ((1 - self.y) * 2 + self.c, d)
        self.up = (g, (self.z + 1) * 2 + self.x)
        self.down = (g, (self.z - 1) * 2 + self.x)
        self.has_up = self.z + 1 < nz
        self.has_down = self.z > 0

    def owner(self, p, x, y, z):
        return ((y * 2 + p) * self.nz + z) * 2 + x

    def greet(self):
        barrier = pltpu.get_barrier_semaphore()

        def tell(to):
            pl.semaphore_signal(barrier, inc=1, device_id=to, device_id_type=MESH)

        tell(self.other)
        tell(self.over_x)
        tell(self.over_y)
        pl.when(self.has_up)(lambda: tell(self.up))
        pl.when(self.has_down)(lambda: tell(self.down))
        peers = 3 + jnp.where(self.has_up, 1, 0) + jnp.where(self.has_down, 1, 0)
        pl.semaphore_wait(barrier, peers)


def remote(src, dst, send, recv, to):
    return pltpu.make_async_remote_copy(
        src_ref=src, dst_ref=dst, send_sem=send, recv_sem=recv, device_id=to, device_id_type=MESH
    )


def gather_kernel(
    slot_in, cov_in, count_in, q_in, k_in, v_in, q_all, k_all, vt, ks, flags, v_all, parcel, arrive, s_up, s_down, s_x, s_y, s_two, s_near, r_near, s_own, s_load, *, nz
):
    me = Place(nz)
    half = q_all.shape[2]
    here = k_in.shape[0]
    keep = pl.ds(pl.multiple_of(me.c * half, half), half)
    give = pl.ds(pl.multiple_of((1 - me.c) * half, half), half)
    mine = pl.ds(me.c * here, here)
    own = me.owner(me.c, me.x, me.y, me.z)
    own_copies = [
        pltpu.make_async_copy(q_in.at[:, keep], q_all.at[own], s_own.at[0]),
        pltpu.make_async_copy(k_in.at[:, :, keep], k_all.at[mine], s_own.at[1]),
        pltpu.make_async_copy(v_in.at[:, :, keep], v_all.at[mine], s_own.at[2]),
    ]
    steps = 2 * nz - 2
    near = []
    for t in range(2 * here):
        to_slot = (k_all, v_all)[t // here].at[me.c * here + t % here]
        near.append(remote(parcel.at[t], to_slot, s_near.at[1 + t], r_near.at[t], me.other))
    own_copies[0].start()
    loads = []
    for t in range(2 * here):
        src = (k_in, v_in)[t // here]
        loads.append(pltpu.make_async_copy(src.at[t % here, :, give], parcel.at[t], s_load.at[t]))
        loads[t].start()
    own_copies[1].start()
    own_copies[2].start()
    me.greet()
    heads = half // HD
    by_head = head_lanes(half)
    near_q = remote(q_in.at[:, give], q_all.at[own], s_near.at[0], arrive.at[own], me.other)
    near_q.start()
    own_copies[0].wait()

    def await_block(idx):
        remote(q_all.at[idx], q_all.at[idx], s_near.at[0], arrive.at[idx], me.over_x).wait_recv()

    def spread(p, i, off, zs):
        idx = me.owner(p, me.x, me.y, zs)
        blk = q_all.at[idx]
        up = remote(blk, blk, s_up.at[p, i], arrive.at[idx], me.up)
        down = remote(blk, blk, s_down.at[p, i], arrive.at[idx], me.down)
        return (
            (jnp.logical_and(off >= 0, me.has_up), up),
            (jnp.logical_and(off <= 0, me.has_down), down),
            (None, remote(blk, blk, s_x.at[p, i], arrive.at[idx], me.over_x)),
            (None, remote(blk, blk, s_y.at[p, i], arrive.at[idx], me.over_y)),
        )

    def begin(copies):
        for cond, copy in copies:
            if cond is None:
                copy.start()
            else:
                pl.when(cond)(copy.start)

    def sent(copies):
        for cond, copy in copies:
            if cond is None:
                copy.wait_send()
            else:
                pl.when(cond)(copy.wait_send)

    begin(spread(me.c, 0, jnp.int32(0), me.z))
    await_block(me.owner(1 - me.c, me.x, me.y, me.z))
    begin(spread(1 - me.c, 0, jnp.int32(0), me.z))

    def source(i):
        off = lax.div(i + 1, 2) * (2 * lax.rem(i, 2) - 1)
        zs = me.z - off
        return off, zs, jnp.logical_and(zs >= 0, zs < nz)

    def second(i, zs):
        a = me.owner(0, 1 - me.x, me.y, zs)
        b = me.owner(1, me.x, 1 - me.y, zs)
        return (
            (a, remote(q_all.at[a], q_all.at[a], s_two.at[0, i], arrive.at[a], me.over_y)),
            (b, remote(q_all.at[b], q_all.at[b], s_two.at[1, i], arrive.at[b], me.over_x)),
        )

    def do_second(i):
        off, zs, ok = source(i)

        @pl.when(ok)
        def _():
            for idx, copy in second(i, zs):
                await_block(idx)
                copy.start()

    def step(i, carry):
        off, zs, ok = source(i)

        @pl.when(ok)
        def _():
            for p in (0, 1):
                await_block(me.owner(p, me.x, me.y, zs))
                begin(spread(p, i, off, zs))

        do_second(i - 1)
        for t in range(2 * here):

            @pl.when(i == 1 + t * steps // (2 * here))
            def _():
                loads[t].wait()
                near[t].start()

        return carry

    count = 2 * nz - 1
    lax.fori_loop(1, count, step, 0)
    do_second(jnp.int32(count - 1))

    def finish(i, carry):
        off, zs, ok = source(i)

        @pl.when(ok)
        def _():
            await_block(me.owner(0, me.x, 1 - me.y, zs))
            await_block(me.owner(1, 1 - me.x, me.y, zs))
            await_block(me.owner(0, 1 - me.x, 1 - me.y, zs))
            await_block(me.owner(1, 1 - me.x, 1 - me.y, zs))
            for p in (0, 1):
                sent(spread(p, i, off, zs))
            for _, copy in second(i, zs):
                copy.wait_send()

        return carry

    slot_id = lax.broadcasted_iota(jnp.int32, cov_in.shape, 1)
    listed = slot_id < count_in[...]
    frame_id = lax.broadcasted_iota(jnp.int32, slot_in.shape, 1)
    lane = lax.broadcasted_iota(jnp.int32, flags.shape, 1)
    found = jnp.zeros(flags.shape, jnp.int32)
    for r in range(2 * here):
        row = ((me.y * 2 + r // here) * nz + me.z) * 2 * here + me.x * here + r % here
        frame = jnp.sum(jnp.where(slot_in[...] == row, frame_id, 0), axis=1, keepdims=True)
        hit = jnp.where(jnp.logical_and(cov_in[...] == frame, listed), 1, 0)
        found = found + jnp.where(lane == r, jnp.max(hit, axis=1, keepdims=True), 0)
    flags[...] = found

    def turn(core):
        def one(t, largest):
            f = core * here + t

            def put(h, part, block):
                vt[f, h, part, :] = block

            turn_values(v_all[f], put, heads)
            return jnp.maximum(largest, largest_square(k_all[f], by_head))

        return one

    own_copies[1].wait()
    own_copies[2].wait()
    largest = lax.fori_loop(0, here, turn(me.c), jnp.zeros((1, 128), jnp.float32))
    for copy in near:
        copy.wait()
    largest = lax.fori_loop(0, here, turn(1 - me.c), largest)
    ks[...] = jnp.broadcast_to(largest, ks.shape)
    lax.fori_loop(0, count, finish, 0)
    near_q.wait_send()


def gather(frame_slot, covisible, counts, q, k, v, devices):
    rows, width = q.shape
    frames, tok, _ = k.shape
    nz = devices // 8
    half = width // 2
    count = 2 * nz - 1
    dma = pltpu.SemaphoreType.DMA
    anywhere = pl.BlockSpec(memory_space=pl.ANY)
    vmem = pl.BlockSpec(memory_space=pltpu.VMEM)
    return pl.pallas_call(
        functools.partial(gather_kernel, nz=nz),
        out_shape=(
            jax.ShapeDtypeStruct((devices, rows, half), q.dtype),
            jax.ShapeDtypeStruct((2 * frames, tok, half), k.dtype),
            jax.ShapeDtypeStruct((2 * frames, half // HD, HD + 16, tok), v.dtype),
            jax.ShapeDtypeStruct((8, 128), jnp.float32),
            jax.ShapeDtypeStruct((covisible.shape[0], 2 * frames), jnp.int32),
        ),
        in_specs=[vmem, vmem, vmem, vmem, anywhere, anywhere],
        out_specs=(vmem,) * 5,
        scratch_shapes=[
            pltpu.VMEM((2 * frames, tok, half), v.dtype),
            pltpu.VMEM((2 * frames, tok, half), k.dtype),
            dma((devices,)),
            dma((2, count)),
            dma((2, count)),
            dma((2, count)),
            dma((2, count)),
            dma((2, count)),
            dma((1 + 2 * frames,)),
            dma((2 * frames,)),
            dma((3,)),
            dma((2 * frames,)),
        ],
        compiler_params=pltpu.CompilerParams(
            collective_id=0, has_side_effects=True, vmem_limit_bytes=VMEM_LIMIT
        ),
        name="gather",
    )(frame_slot[None, :], covisible, counts[:, None], q, k, v)


def expander(heads, first, width):
    r = lax.broadcasted_iota(jnp.int32, (STAT, width), 0)
    col = lax.broadcasted_iota(jnp.int32, (STAT, width), 1)
    head = jnp.where(col < heads * HD, lax.div(col, HD), col - heads * HD - heads)
    head = jnp.where(head < 0, -STAT, jnp.where(head < heads, head, -STAT))
    return jnp.where(head + first == r, 1.0, 0.0).astype(jnp.bfloat16)


def scatter_kernel(
    msg, out, r_one, r_two, r_up, r_down, b_two, b_z, kept, att, exp_ref, exp_tot,
    sem_one, sem_two, sem_up, sem_down, s_one, s_two, s_z, sem_last, *, nz, heads
):
    me = Place(nz)
    width = heads * HD
    rows = msg.shape[1]
    count = 2 * nz - 1
    exp_ref[...] = expander(heads, 0, width + STAT)
    exp_tot[...] = expander(heads, heads, width)
    me.greet()
    lane = lax.broadcasted_iota(jnp.int32, (rows, STAT), 1)

    def target(i):
        off = lax.div(count - i, 2) * (1 - 2 * lax.rem(i, 2))
        zd = me.z + off
        return off, zd, jnp.logical_and(zd >= 0, zd < nz)

    def merge(parts):
        parts = [part.astype(jnp.float32) for part in parts]
        stats = [part[:, width:] for part in parts]
        top = functools.reduce(jnp.maximum, stats)
        total = None
        for part, st in zip(parts, stats):
            factor = jnp.exp2(st - top).astype(jnp.bfloat16)
            wide = jnp.dot(factor, exp_ref[...], preferred_element_type=jnp.float32)
            total = part * wide if total is None else total + part * wide
        tail = jnp.where(lane < heads, top, total[:, width:])
        return jnp.concatenate([total[:, :width], tail], axis=1)

    def ones(i, zd):
        a0 = me.owner(0, 1 - me.x, 1 - me.y, zd)
        a1 = me.owner(0, me.x, 1 - me.y, zd)
        b0 = me.owner(1, 1 - me.x, 1 - me.y, zd)
        b1 = me.owner(1, 1 - me.x, me.y, zd)
        return tuple(
            remote(msg.at[src], r_one.at[p, k, zd], s_one.at[p, k, zd], sem_one.at[p, k, zd], to)
            for p, k, src, to in (
                (0, 0, a0, me.over_y), (1, 0, b0, me.over_x), (0, 1, a1, me.over_y), (1, 1, b1, me.over_x)
            )
        )

    def first(i, carry):
        off, zd, ok = target(i)

        @pl.when(ok)
        def _():
            for copy in ones(i, zd):
                copy.start()

        return carry

    lax.fori_loop(0, count, first, 0)

    def twos(zd):
        return tuple(
            remote(b_two.at[p, zd], r_two.at[p, zd], s_two.at[p, zd], sem_two.at[p, zd], to)
            for p, to in ((0, me.over_x), (1, me.over_y))
        )

    def second(i):
        off, zd, ok = target(i)

        @pl.when(ok)
        def _():
            waits = ones(i, zd)
            copies = twos(zd)
            for p in (0, 1):
                waits[p].wait_recv()
                src = me.owner(0, 1 - me.x, me.y, zd) if p == 0 else me.owner(1, me.x, 1 - me.y, zd)
                b_two[p, zd] = merge([msg[src], r_one[p, 0, zd]]).astype(jnp.bfloat16)
                copies[p].start()

    def z_copies(p, zd):
        return (
            remote(b_z.at[p, zd], r_up.at[p, zd], s_z.at[p, zd], sem_up.at[p, zd], me.up),
            remote(b_z.at[p, zd], r_down.at[p, zd], s_z.at[p, zd], sem_down.at[p, zd], me.down),
        )

    def third(i):
        off, zd, ok = target(i)

        @pl.when(ok)
        def _():
            waits = ones(i, zd)
            two = twos(zd)
            for p in (0, 1):
                up, down = z_copies(p, zd)
                waits[2 + p].wait_recv()
                two[p].wait_recv()
                here = merge([msg[me.owner(p, me.x, me.y, zd)], r_one[p, 1, zd], r_two[p, zd]])
                kept[p] = here

                @pl.when(jnp.logical_and(off >= 0, me.has_down))
                def _():
                    up.wait_recv()
                    kept[p] = merge([kept[p], r_up[p, zd]])

                @pl.when(jnp.logical_and(off <= 0, me.has_up))
                def _():
                    down.wait_recv()
                    kept[p] = merge([kept[p], r_down[p, zd]])

                @pl.when(off != 0)
                def _():
                    b_z[p, zd] = kept[p].astype(jnp.bfloat16)

                pl.when(off > 0)(up.start)
                pl.when(off < 0)(down.start)

    def step(i, carry):
        second(i)
        pl.when(i > 0)(lambda: third(i - 1))
        return carry

    lax.fori_loop(0, count, step, 0)
    third(jnp.int32(count - 1))

    for p in (0, 1):
        full = kept[p]
        tail = full[:, width:]
        inverse = 1.0 / jnp.where(jnp.logical_and(lane >= heads, lane < 2 * heads), tail, 1.0)
        hi = inverse.astype(jnp.bfloat16)
        lo = (inverse - hi.astype(jnp.float32)).astype(jnp.bfloat16)
        wide = jnp.dot(hi, exp_tot[...], preferred_element_type=jnp.float32)
        wide = wide + jnp.dot(lo, exp_tot[...], preferred_element_type=jnp.float32)
        att[p] = (full[:, :width] * wide).astype(jnp.bfloat16)
    last = remote(att.at[1 - me.c], out.at[me.c], sem_last.at[0], sem_last.at[1], me.other)
    last.start()
    out[me.c] = att[me.c]

    def finish(i, carry):
        off, zd, ok = target(i)

        @pl.when(ok)
        def _():
            for copy in ones(i, zd):
                copy.wait_send()
            for copy in twos(zd):
                copy.wait_send()
            for p in (0, 1):
                up, down = z_copies(p, zd)
                pl.when(off > 0)(up.wait_send)
                pl.when(off < 0)(down.wait_send)

        return carry

    lax.fori_loop(0, count, finish, 0)
    last.wait()


def scatter(msg, heads):
    devices, rows, wide = msg.shape
    nz = devices // 8
    width = heads * HD
    dma = pltpu.SemaphoreType.DMA
    vmem = pl.BlockSpec(memory_space=pltpu.VMEM)
    block = (rows, wide)
    return pl.pallas_call(
        functools.partial(scatter_kernel, nz=nz, heads=heads),
        out_shape=jax.ShapeDtypeStruct((2, rows, width), jnp.bfloat16),
        in_specs=[vmem],
        out_specs=vmem,
        scratch_shapes=[
            pltpu.VMEM((2, 2, nz) + block, jnp.bfloat16),
            pltpu.VMEM((2, nz) + block, jnp.bfloat16),
            pltpu.VMEM((2, nz) + block, jnp.bfloat16),
            pltpu.VMEM((2, nz) + block, jnp.bfloat16),
            pltpu.VMEM((2, nz) + block, jnp.bfloat16),
            pltpu.VMEM((2, nz) + block, jnp.bfloat16),
            pltpu.VMEM((2,) + block, jnp.float32),
            pltpu.VMEM((2, rows, width), jnp.bfloat16),
            pltpu.VMEM((STAT, wide), jnp.bfloat16),
            pltpu.VMEM((STAT, width), jnp.bfloat16),
            dma((2, 2, nz)),
            dma((2, nz)),
            dma((2, nz)),
            dma((2, nz)),
            dma((2, 2, nz)),
            dma((2, nz)),
            dma((2, nz)),
            dma((2,)),
        ],
        compiler_params=pltpu.CompilerParams(
            collective_id=1, has_side_effects=True, vmem_limit_bytes=VMEM_LIMIT
        ),
        name="scatter",
    )(msg)


def needed_frames(rows, frame_slot, covisible, counts):
    frame_ids = jnp.arange(frame_slot.shape[0], dtype=jnp.int32)
    hits = frame_slot[None, :] == rows[:, None]
    frames = jnp.sum(jnp.where(hits, frame_ids[None, :], 0), axis=1)
    in_list = jnp.arange(covisible.shape[1], dtype=jnp.int32)[None, :] < counts[:, None]
    match = (covisible[:, :, None] == frames[None, None, :]) & in_list[:, :, None]
    return jnp.any(match, axis=1).astype(jnp.int32)


def body_cores(devices, queries, keys, values, frame_slot, covisible, counts, out_weight):
    here, tok, width = keys.shape
    heads = width // HD // 2
    q_all, k_all, vt, key_square, flags = gather(frame_slot, covisible, counts, queries, keys, values, devices)
    own = queries.shape[0]
    msg = attend(flags, q_all.reshape(devices * own, width // 2), k_all, vt, key_square)
    halves = scatter(msg.reshape(devices, own, -1), heads)
    weight = out_weight.reshape(2, width // 2, -1)
    return jnp.einsum("hrd,hde->re", halves, weight, preferred_element_type=jnp.float32).astype(jnp.bfloat16)


def body_any(queries, keys, values, frame_slot, covisible, counts, out_weight):
    axes = ("group", "dev")
    here, tok, width = keys.shape
    heads = width // HD
    rows = jnp.arange(here, dtype=jnp.int32) + lax.axis_index(axes) * here
    flags = needed_frames(rows, frame_slot, covisible, counts)
    q_all = lax.all_gather(queries, axes, axis=0, tiled=True)
    msg = attend(flags, q_all, keys, *prepare(keys, values)).astype(jnp.float32)
    top = msg[:, width : width + heads]
    totals = msg[:, width + heads : width + 2 * heads]
    factor = jnp.exp2(top - lax.pmax(top, axes))
    numer = msg[:, :width] * jnp.repeat(factor, HD, axis=1)
    own_numer = lax.psum_scatter(numer, axes, scatter_dimension=0, tiled=True)
    own_totals = lax.psum_scatter(totals * factor, axes, scatter_dimension=0, tiled=True)
    attended = (own_numer / jnp.repeat(own_totals, HD, axis=1)).astype(jnp.bfloat16)
    return jnp.dot(attended, out_weight, preferred_element_type=jnp.float32).astype(jnp.bfloat16)


def solution(mesh):
    group, dev = mesh.shape["group"], mesh.shape["dev"]
    body = body_any
    if group == 4 and dev % 2 == 0:
        body = functools.partial(body_cores, group * dev)
    return jax.shard_map(
        body,
        mesh=mesh,
        in_specs=(
            P(("group", "dev"), None),
            P(("group", "dev"), None, None),
            P(("group", "dev"), None, None),
            P(),
            P(),
            P(),
            P(),
        ),
        out_specs=P(("group", "dev"), None),
        check_vma=False,
    )
```

```python
import functools

import jax
import jax.numpy as jnp
from jax import lax
from jax.experimental import pallas as pl
from jax.experimental.pallas import tpu as pltpu
from jax.sharding import PartitionSpec as P

HD = 64
NEG_FILL = -1e30
LOG2E = 1.4426950408889634
MESH = pl.DeviceIdType.MESH
STAT = 128
TOP_STEP = 8.0
SMALL = 60.0
VMEM_LIMIT = 56 * 1024 * 1024


def head_lanes(width):
    row_id = lax.broadcasted_iota(jnp.int32, (width, 128), 0)
    col_id = lax.broadcasted_iota(jnp.int32, (width, 128), 1)
    return jnp.where(lax.div(row_id, HD) == col_id, 1.0, 0.0).astype(jnp.bfloat16)


def largest_square(block, by_head):
    squares = jnp.dot(block * block, by_head, preferred_element_type=jnp.float32)
    return jnp.max(squares, axis=0, keepdims=True)


def turn_values(block, put, heads):
    turned = block.T
    for h in range(heads):
        put(h, slice(0, HD), turned[h * HD : (h + 1) * HD, :])
        put(h, slice(HD, HD + 16), jnp.ones((16, block.shape[0]), block.dtype))


def attend_kernel(flags, q_ref, k_ref, vt, ks_ref, out_ref, qt, acc, stat, *, heads, frames, tok, qframes):
    width = heads * HD
    scale = LOG2E * HD ** (-0.5)

    by_head = head_lanes(width)
    key_square = ks_ref[0:1, :]
    stat[...] = jnp.zeros_like(stat)
    qt[...] = jnp.zeros_like(qt)

    def one_query(qi, carry):
        rows = pl.ds(pl.multiple_of(qi * tok, tok), tok)
        for g in range(heads // 2):
            pair = q_ref[rows, g * 128 : (g + 1) * 128].T
            pair = pair * jnp.asarray(HD ** (-0.5), pair.dtype)
            qt[2 * g, 0:HD, :] = pair[0:HD, :]
            qt[2 * g + 1, HD:128, :] = pair[HD:128, :]
        acc[...] = jnp.zeros_like(acc)
        stat[0:heads, :] = jnp.full((heads, tok), NEG_FILL, jnp.float32)
        bound = jnp.max(largest_square(q_ref[rows, :], by_head) * key_square) * (scale * scale)
        small = bound <= SMALL * SMALL

        def scores(f, h):
            kp = k_ref[f, :, (h // 2) * 128 : (h // 2 + 1) * 128]
            return jnp.dot(kp, qt[h], preferred_element_type=jnp.float32)

        def small_frame(f):
            stat[0:heads, :] = jnp.zeros((heads, tok), jnp.float32)

            def weigh(s):
                return jnp.exp(s).astype(jnp.bfloat16)

            def add(h, p):
                acc[h] += jnp.dot(vt[f, h], p, preferred_element_type=jnp.float32)

            s, p = scores(f, 0), None
            for h in range(heads):
                later = scores(f, h + 1) if h + 1 < heads else None
                now = weigh(s)
                if h > 0:
                    add(h - 1, p)
                s, p = later, now
            add(heads - 1, p)

        def any_frame(f):
            for h in range(heads):
                s = scores(f, h)
                top = jnp.max(s, axis=0, keepdims=True) * LOG2E
                old = stat[h : h + 1, :]
                new = jnp.maximum(old, jnp.ceil(top * (1.0 / TOP_STEP)) * TOP_STEP)
                p = jnp.exp2(s * LOG2E - new).astype(jnp.bfloat16)
                add = jnp.dot(vt[f, h], p, preferred_element_type=jnp.float32)
                acc[h] = acc[h] * jnp.exp2(old - new) + add
                stat[h : h + 1, :] = new

        def one_frame(f, c):
            needed = flags[qi, f] != 0
            pl.when(jnp.logical_and(needed, small))(lambda: small_frame(f))
            pl.when(jnp.logical_and(needed, jnp.logical_not(small)))(lambda: any_frame(f))
            return c

        lax.fori_loop(0, frames, one_frame, 0)
        for h in range(heads):
            stat[heads + h : heads + h + 1, :] = acc[h, HD : HD + 1, :]
        stats = jnp.concatenate([stat[...]] * (STAT // (2 * heads)), axis=0)
        for g in range(heads // 2):
            both = jnp.concatenate([acc[2 * g, 0:HD, :], acc[2 * g + 1, 0:HD, :]], axis=0)
            out_ref[rows, g * 128 : (g + 1) * 128] = both.astype(jnp.bfloat16).T
        out_ref[rows, width : width + STAT] = stats.astype(jnp.bfloat16).T
        return carry

    lax.fori_loop(0, qframes, one_query, 0)


def attend(flags, q, k, vt, key_square):
    rows, width = q.shape
    frames, tok = k.shape[0], k.shape[1]
    heads = width // HD
    qframes = rows // tok
    return pl.pallas_call(
        functools.partial(attend_kernel, heads=heads, frames=frames, tok=tok, qframes=qframes),
        out_shape=jax.ShapeDtypeStruct((rows, width + STAT), jnp.bfloat16),
        in_specs=[pl.BlockSpec(memory_space=pltpu.SMEM)] + [pl.BlockSpec(memory_space=pltpu.VMEM)] * 4,
        out_specs=pl.BlockSpec(memory_space=pltpu.VMEM),
        scratch_shapes=[
            pltpu.VMEM((heads, 128, tok), jnp.bfloat16),
            pltpu.VMEM((heads, HD + 16, tok), jnp.float32),
            pltpu.VMEM((2 * heads, tok), jnp.float32),
        ],
        compiler_params=pltpu.CompilerParams(vmem_limit_bytes=VMEM_LIMIT),
        name="attend",
    )(flags, q, k, vt, key_square)


def prepare_kernel(k_ref, v_ref, vt, ks_ref, *, heads, frames):
    by_head = head_lanes(k_ref.shape[2])

    def one(f, largest):
        def put(h, part, block):
            vt[f, h, part, :] = block

        turn_values(v_ref[f], put, heads)
        return jnp.maximum(largest, largest_square(k_ref[f], by_head))

    largest = lax.fori_loop(0, frames, one, jnp.zeros((1, 128), jnp.float32))
    ks_ref[...] = jnp.broadcast_to(largest, ks_ref.shape)


def prepare(k, v):
    frames, tok, width = k.shape
    heads = width // HD
    return pl.pallas_call(
        functools.partial(prepare_kernel, heads=heads, frames=frames),
        out_shape=(
            jax.ShapeDtypeStruct((frames, heads, HD + 16, tok), v.dtype),
            jax.ShapeDtypeStruct((8, 128), jnp.float32),
        ),
        compiler_params=pltpu.CompilerParams(vmem_limit_bytes=VMEM_LIMIT),
        name="prepare",
    )(k, v)


class Place:
    def __init__(self, nz):
        g, d = lax.axis_index("group"), lax.axis_index("dev")
        self.nz = nz
        self.y, self.c = lax.div(g, 2), lax.rem(g, 2)
        self.z, self.x = lax.div(d, 2), lax.rem(d, 2)
        self.other = (self.y * 2 + 1 - self.c, d)
        self.over_x = (g, self.z * 2 + 1 - self.x)
        self.over_y = ((1 - self.y) * 2 + self.c, d)
        self.up = (g, (self.z + 1) * 2 + self.x)
        self.down = (g, (self.z - 1) * 2 + self.x)
        self.has_up = self.z + 1 < nz
        self.has_down = self.z > 0

    def owner(self, p, x, y, z):
        return ((y * 2 + p) * self.nz + z) * 2 + x

    def greet(self):
        barrier = pltpu.get_barrier_semaphore()

        def tell(to):
            pl.semaphore_signal(barrier, inc=1, device_id=to, device_id_type=MESH)

        tell(self.other)
        tell(self.over_x)
        tell(self.over_y)
        pl.when(self.has_up)(lambda: tell(self.up))
        pl.when(self.has_down)(lambda: tell(self.down))
        peers = 3 + jnp.where(self.has_up, 1, 0) + jnp.where(self.has_down, 1, 0)
        pl.semaphore_wait(barrier, peers)


def remote(src, dst, send, recv, to):
    return pltpu.make_async_remote_copy(
        src_ref=src, dst_ref=dst, send_sem=send, recv_sem=recv, device_id=to, device_id_type=MESH
    )


def gather_kernel(
    slot_in, cov_in, count_in, q_in, k_in, v_in, q_all, k_all, vt, ks, flags, v_all, parcel, arrive, s_up, s_down, s_x, s_y, s_two, s_near, r_near, s_own, s_load, *, nz
):
    me = Place(nz)
    half = q_all.shape[2]
    here = k_in.shape[0]
    keep = pl.ds(pl.multiple_of(me.c * half, half), half)
    give = pl.ds(pl.multiple_of((1 - me.c) * half, half), half)
    mine = pl.ds(me.c * here, here)
    own = me.owner(me.c, me.x, me.y, me.z)
    own_copies = [
        pltpu.make_async_copy(q_in.at[:, keep], q_all.at[own], s_own.at[0]),
        pltpu.make_async_copy(k_in.at[:, :, keep], k_all.at[mine], s_own.at[1]),
        pltpu.make_async_copy(v_in.at[:, :, keep], v_all.at[mine], s_own.at[2]),
    ]
    steps = 2 * nz - 2
    near = []
    for t in range(2 * here):
        to_slot = (k_all, v_all)[t // here].at[me.c * here + t % here]
        near.append(remote(parcel.at[t], to_slot, s_near.at[1 + t], r_near.at[t], me.other))
    own_copies[0].start()
    loads = []
    for t in range(2 * here):
        src = (k_in, v_in)[t // here]
        loads.append(pltpu.make_async_copy(src.at[t % here, :, give], parcel.at[t], s_load.at[t]))
        loads[t].start()
    own_copies[1].start()
    own_copies[2].start()
    me.greet()
    heads = half // HD
    by_head = head_lanes(half)
    near_q = remote(q_in.at[:, give], q_all.at[own], s_near.at[0], arrive.at[own], me.other)
    near_q.start()
    own_copies[0].wait()

    def await_block(idx):
        remote(q_all.at[idx], q_all.at[idx], s_near.at[0], arrive.at[idx], me.over_x).wait_recv()

    def spread(p, i, off, zs):
        idx = me.owner(p, me.x, me.y, zs)
        blk = q_all.at[idx]
        up = remote(blk, blk, s_up.at[p, i], arrive.at[idx], me.up)
        down = remote(blk, blk, s_down.at[p, i], arrive.at[idx], me.down)
        return (
            (jnp.logical_and(off >= 0, me.has_up), up),
            (jnp.logical_and(off <= 0, me.has_down), down),
            (None, remote(blk, blk, s_x.at[p, i], arrive.at[idx], me.over_x)),
            (None, remote(blk, blk, s_y.at[p, i], arrive.at[idx], me.over_y)),
        )

    def begin(copies):
        for cond, copy in copies:
            if cond is None:
                copy.start()
            else:
                pl.when(cond)(copy.start)

    def sent(copies):
        for cond, copy in copies:
            if cond is None:
                copy.wait_send()
            else:
                pl.when(cond)(copy.wait_send)

    begin(spread(me.c, 0, jnp.int32(0), me.z))
    await_block(me.owner(1 - me.c, me.x, me.y, me.z))
    begin(spread(1 - me.c, 0, jnp.int32(0), me.z))

    def source(i):
        off = lax.div(i + 1, 2) * (2 * lax.rem(i, 2) - 1)
        zs = me.z - off
        return off, zs, jnp.logical_and(zs >= 0, zs < nz)

    def second(i, zs):
        a = me.owner(0, 1 - me.x, me.y, zs)
        b = me.owner(1, me.x, 1 - me.y, zs)
        return (
            (a, remote(q_all.at[a], q_all.at[a], s_two.at[0, i], arrive.at[a], me.over_y)),
            (b, remote(q_all.at[b], q_all.at[b], s_two.at[1, i], arrive.at[b], me.over_x)),
        )

    def do_second(i):
        off, zs, ok = source(i)

        @pl.when(ok)
        def _():
            for idx, copy in second(i, zs):
                await_block(idx)
                copy.start()

    def step(i, carry):
        off, zs, ok = source(i)

        @pl.when(ok)
        def _():
            for p in (0, 1):
                await_block(me.owner(p, me.x, me.y, zs))
                begin(spread(p, i, off, zs))

        do_second(i - 1)
        for t in range(2 * here):

            @pl.when(i == 1 + t * steps // (2 * here))
            def _():
                loads[t].wait()
                near[t].start()

        return carry

    count = 2 * nz - 1
    lax.fori_loop(1, count, step, 0)
    do_second(jnp.int32(count - 1))

    def finish(i, carry):
        off, zs, ok = source(i)

        @pl.when(ok)
        def _():
            await_block(me.owner(0, me.x, 1 - me.y, zs))
            await_block(me.owner(1, 1 - me.x, me.y, zs))
            await_block(me.owner(0, 1 - me.x, 1 - me.y, zs))
            await_block(me.owner(1, 1 - me.x, 1 - me.y, zs))
            for p in (0, 1):
                sent(spread(p, i, off, zs))
            for _, copy in second(i, zs):
                copy.wait_send()

        return carry

    slot_id = lax.broadcasted_iota(jnp.int32, cov_in.shape, 1)
    listed = slot_id < count_in[...]
    frame_id = lax.broadcasted_iota(jnp.int32, slot_in.shape, 1)
    lane = lax.broadcasted_iota(jnp.int32, flags.shape, 1)
    found = jnp.zeros(flags.shape, jnp.int32)
    for r in range(2 * here):
        row = ((me.y * 2 + r // here) * nz + me.z) * 2 * here + me.x * here + r % here
        frame = jnp.sum(jnp.where(slot_in[...] == row, frame_id, 0), axis=1, keepdims=True)
        hit = jnp.where(jnp.logical_and(cov_in[...] == frame, listed), 1, 0)
        found = found + jnp.where(lane == r, jnp.max(hit, axis=1, keepdims=True), 0)
    flags[...] = found

    def turn(core):
        def one(t, largest):
            f = core * here + t

            def put(h, part, block):
                vt[f, h, part, :] = block

            turn_values(v_all[f], put, heads)
            return jnp.maximum(largest, largest_square(k_all[f], by_head))

        return one

    own_copies[1].wait()
    own_copies[2].wait()
    largest = lax.fori_loop(0, here, turn(me.c), jnp.zeros((1, 128), jnp.float32))
    for copy in near:
        copy.wait()
    largest = lax.fori_loop(0, here, turn(1 - me.c), largest)
    ks[...] = jnp.broadcast_to(largest, ks.shape)
    lax.fori_loop(0, count, finish, 0)
    near_q.wait_send()


def gather(frame_slot, covisible, counts, q, k, v, devices):
    rows, width = q.shape
    frames, tok, _ = k.shape
    nz = devices // 8
    half = width // 2
    count = 2 * nz - 1
    dma = pltpu.SemaphoreType.DMA
    anywhere = pl.BlockSpec(memory_space=pl.ANY)
    vmem = pl.BlockSpec(memory_space=pltpu.VMEM)
    return pl.pallas_call(
        functools.partial(gather_kernel, nz=nz),
        out_shape=(
            jax.ShapeDtypeStruct((devices, rows, half), q.dtype),
            jax.ShapeDtypeStruct((2 * frames, tok, half), k.dtype),
            jax.ShapeDtypeStruct((2 * frames, half // HD, HD + 16, tok), v.dtype),
            jax.ShapeDtypeStruct((8, 128), jnp.float32),
            jax.ShapeDtypeStruct((covisible.shape[0], 2 * frames), jnp.int32),
        ),
        in_specs=[vmem, vmem, vmem, vmem, anywhere, anywhere],
        out_specs=(vmem,) * 5,
        scratch_shapes=[
            pltpu.VMEM((2 * frames, tok, half), v.dtype),
            pltpu.VMEM((2 * frames, tok, half), k.dtype),
            dma((devices,)),
            dma((2, count)),
            dma((2, count)),
            dma((2, count)),
            dma((2, count)),
            dma((2, count)),
            dma((1 + 2 * frames,)),
            dma((2 * frames,)),
            dma((3,)),
            dma((2 * frames,)),
        ],
        compiler_params=pltpu.CompilerParams(
            collective_id=0, has_side_effects=True, vmem_limit_bytes=VMEM_LIMIT
        ),
        name="gather",
    )(frame_slot[None, :], covisible, counts[:, None], q, k, v)


def expander(heads, first, width):
    r = lax.broadcasted_iota(jnp.int32, (STAT, width), 0)
    col = lax.broadcasted_iota(jnp.int32, (STAT, width), 1)
    in_stat = lax.rem(jnp.maximum(col - heads * HD, 0), 2 * heads) - heads
    head = jnp.where(col < heads * HD, lax.div(col, HD), in_stat)
    head = jnp.where(head < 0, -STAT, jnp.where(head < heads, head, -STAT))
    return jnp.where(head + first == r, 1.0, 0.0).astype(jnp.bfloat16)


def scatter_kernel(
    msg, out, r_one, r_two, r_up, r_down, b_two, b_z, kept, att, exp_ref, exp_tot, copies_of, b_stat, r_stat,
    s_stat, sem_stat, sem_one, sem_two, sem_up, sem_down, s_one, s_two, s_z, sem_last, *, nz, heads
):
    me = Place(nz)
    width = heads * HD
    rows = msg.shape[1]
    count = 2 * nz - 1
    exp_ref[...] = expander(heads, 0, width + STAT)
    exp_tot[...] = expander(heads, heads, width)
    r_id = lax.broadcasted_iota(jnp.int32, (STAT, STAT), 0)
    c_id = lax.broadcasted_iota(jnp.int32, (STAT, STAT), 1)
    same = lax.rem(r_id, 2 * heads) == lax.rem(c_id, 2 * heads)
    copies_of[...] = jnp.where(same, 1.0, 0.0).astype(jnp.bfloat16)
    lane = lax.broadcasted_iota(jnp.int32, (rows, STAT), 1)
    slot = lax.div(lane, 2 * heads)
    lane = lax.rem(lane, 2 * heads)

    def one_target(p, k, zd):
        if k == 0:
            return me.owner(p, 1 - me.x, 1 - me.y, zd)
        return me.owner(0, me.x, 1 - me.y, zd) if p == 0 else me.owner(1, 1 - me.x, me.y, zd)

    for p in (0, 1):
        packed = jnp.zeros((rows, STAT), jnp.float32)
        for k in (0, 1):
            for zd in range(nz):
                stats = msg[one_target(p, k, zd), :, width:].astype(jnp.float32)
                packed = jnp.where(slot == k * nz + zd, stats, packed)
        b_stat[p] = packed.astype(jnp.bfloat16)
    me.greet()
    stat_copies = [
        remote(b_stat.at[p], r_stat.at[p], s_stat.at[p], sem_stat.at[p], to)
        for p, to in ((0, me.over_y), (1, me.over_x))
    ]

    def joined(p, k, zd):
        picked = jnp.where(slot == k * nz + zd, r_stat[p].astype(jnp.float32), 0.0).astype(jnp.bfloat16)
        stats = jnp.dot(picked, copies_of[...], preferred_element_type=jnp.float32)
        return jnp.concatenate([r_one[p, k, zd].astype(jnp.float32), stats], axis=1)

    def target(i):
        off = lax.div(count - i, 2) * (1 - 2 * lax.rem(i, 2))
        zd = me.z + off
        return off, zd, jnp.logical_and(zd >= 0, zd < nz)

    def merge(parts):
        parts = [part.astype(jnp.float32) for part in parts]
        stats = [part[:, width:] for part in parts]
        top = functools.reduce(jnp.maximum, stats)
        total = None
        for part, st in zip(parts, stats):
            factor = jnp.exp2(st - top).astype(jnp.bfloat16)
            wide = jnp.dot(factor, exp_ref[...], preferred_element_type=jnp.float32)
            total = part * wide if total is None else total + part * wide
        tail = jnp.where(lane < heads, top, total[:, width:])
        return jnp.concatenate([total[:, :width], tail], axis=1)

    def ones(i, zd):
        return tuple(
            remote(
                msg.at[one_target(p, k, zd), :, 0:width],
                r_one.at[p, k, zd],
                s_one.at[p, k, zd],
                sem_one.at[p, k, zd],
                (me.over_y, me.over_x)[p],
            )
            for k in (0, 1)
            for p in (0, 1)
        )

    def first(i, carry):
        off, zd, ok = target(i)

        @pl.when(ok)
        def _():
            for copy in ones(i, zd):
                copy.start()

        return carry

    for copy in stat_copies:
        copy.start()
    lax.fori_loop(0, count, first, 0)
    for copy in stat_copies:
        copy.wait_recv()

    def twos(zd):
        return tuple(
            remote(b_two.at[p, zd], r_two.at[p, zd], s_two.at[p, zd], sem_two.at[p, zd], to)
            for p, to in ((0, me.over_x), (1, me.over_y))
        )

    def second(i):
        off, zd, ok = target(i)

        @pl.when(ok)
        def _():
            waits = ones(i, zd)
            copies = twos(zd)
            for p in (0, 1):
                waits[p].wait_recv()
                src = me.owner(0, 1 - me.x, me.y, zd) if p == 0 else me.owner(1, me.x, 1 - me.y, zd)
                b_two[p, zd] = merge([msg[src], joined(p, 0, zd)]).astype(jnp.bfloat16)
                copies[p].start()

    def z_copies(p, zd):
        return (
            remote(b_z.at[p, zd], r_up.at[p, zd], s_z.at[p, zd], sem_up.at[p, zd], me.up),
            remote(b_z.at[p, zd], r_down.at[p, zd], s_z.at[p, zd], sem_down.at[p, zd], me.down),
        )

    def third(i):
        off, zd, ok = target(i)

        @pl.when(ok)
        def _():
            waits = ones(i, zd)
            two = twos(zd)
            for p in (0, 1):
                up, down = z_copies(p, zd)
                waits[2 + p].wait_recv()
                two[p].wait_recv()
                here = merge([msg[me.owner(p, me.x, me.y, zd)], joined(p, 1, zd), r_two[p, zd]])
                kept[p] = here

                @pl.when(jnp.logical_and(off >= 0, me.has_down))
                def _():
                    up.wait_recv()
                    kept[p] = merge([kept[p], r_up[p, zd]])

                @pl.when(jnp.logical_and(off <= 0, me.has_up))
                def _():
                    down.wait_recv()
                    kept[p] = merge([kept[p], r_down[p, zd]])

                @pl.when(off != 0)
                def _():
                    b_z[p, zd] = kept[p].astype(jnp.bfloat16)

                pl.when(off > 0)(up.start)
                pl.when(off < 0)(down.start)

    def step(i, carry):
        second(i)
        pl.when(i > 0)(lambda: third(i - 1))
        return carry

    lax.fori_loop(0, count, step, 0)
    third(jnp.int32(count - 1))

    for p in (0, 1):
        full = kept[p]
        tail = full[:, width:]
        inverse = 1.0 / jnp.where(jnp.logical_and(lane >= heads, lane < 2 * heads), tail, 1.0)
        hi = inverse.astype(jnp.bfloat16)
        lo = (inverse - hi.astype(jnp.float32)).astype(jnp.bfloat16)
        wide = jnp.dot(hi, exp_tot[...], preferred_element_type=jnp.float32)
        wide = wide + jnp.dot(lo, exp_tot[...], preferred_element_type=jnp.float32)
        att[p] = (full[:, :width] * wide).astype(jnp.bfloat16)
    last = remote(att.at[1 - me.c], out.at[me.c], sem_last.at[0], sem_last.at[1], me.other)
    last.start()
    out[me.c] = att[me.c]

    def finish(i, carry):
        off, zd, ok = target(i)

        @pl.when(ok)
        def _():
            for copy in ones(i, zd):
                copy.wait_send()
            for copy in twos(zd):
                copy.wait_send()
            for p in (0, 1):
                up, down = z_copies(p, zd)
                pl.when(off > 0)(up.wait_send)
                pl.when(off < 0)(down.wait_send)

        return carry

    lax.fori_loop(0, count, finish, 0)
    for copy in stat_copies:
        copy.wait_send()
    last.wait()


def scatter(msg, heads):
    devices, rows, wide = msg.shape
    nz = devices // 8
    width = heads * HD
    dma = pltpu.SemaphoreType.DMA
    vmem = pl.BlockSpec(memory_space=pltpu.VMEM)
    block = (rows, wide)
    return pl.pallas_call(
        functools.partial(scatter_kernel, nz=nz, heads=heads),
        out_shape=jax.ShapeDtypeStruct((2, rows, width), jnp.bfloat16),
        in_specs=[vmem],
        out_specs=vmem,
        scratch_shapes=[
            pltpu.VMEM((2, 2, nz, rows, width), jnp.bfloat16),
            pltpu.VMEM((2, nz) + block, jnp.bfloat16),
            pltpu.VMEM((2, nz) + block, jnp.bfloat16),
            pltpu.VMEM((2, nz) + block, jnp.bfloat16),
            pltpu.VMEM((2, nz) + block, jnp.bfloat16),
            pltpu.VMEM((2, nz) + block, jnp.bfloat16),
            pltpu.VMEM((2,) + block, jnp.float32),
            pltpu.VMEM((2, rows, width), jnp.bfloat16),
            pltpu.VMEM((STAT, wide), jnp.bfloat16),
            pltpu.VMEM((STAT, width), jnp.bfloat16),
            pltpu.VMEM((STAT, STAT), jnp.bfloat16),
            pltpu.VMEM((2, rows, STAT), jnp.bfloat16),
            pltpu.VMEM((2, rows, STAT), jnp.bfloat16),
            dma((2,)),
            dma((2,)),
            dma((2, 2, nz)),
            dma((2, nz)),
            dma((2, nz)),
            dma((2, nz)),
            dma((2, 2, nz)),
            dma((2, nz)),
            dma((2, nz)),
            dma((2,)),
        ],
        compiler_params=pltpu.CompilerParams(
            collective_id=1, has_side_effects=True, vmem_limit_bytes=VMEM_LIMIT
        ),
        name="scatter",
    )(msg)


def needed_frames(rows, frame_slot, covisible, counts):
    frame_ids = jnp.arange(frame_slot.shape[0], dtype=jnp.int32)
    hits = frame_slot[None, :] == rows[:, None]
    frames = jnp.sum(jnp.where(hits, frame_ids[None, :], 0), axis=1)
    in_list = jnp.arange(covisible.shape[1], dtype=jnp.int32)[None, :] < counts[:, None]
    match = (covisible[:, :, None] == frames[None, None, :]) & in_list[:, :, None]
    return jnp.any(match, axis=1).astype(jnp.int32)


def body_cores(devices, queries, keys, values, frame_slot, covisible, counts, out_weight):
    here, tok, width = keys.shape
    heads = width // HD // 2
    q_all, k_all, vt, key_square, flags = gather(frame_slot, covisible, counts, queries, keys, values, devices)
    own = queries.shape[0]
    msg = attend(flags, q_all.reshape(devices * own, width // 2), k_all, vt, key_square)
    halves = scatter(msg.reshape(devices, own, -1), heads)
    weight = out_weight.reshape(2, width // 2, -1)
    return jnp.einsum("hrd,hde->re", halves, weight, preferred_element_type=jnp.float32).astype(jnp.bfloat16)


def body_any(queries, keys, values, frame_slot, covisible, counts, out_weight):
    axes = ("group", "dev")
    here, tok, width = keys.shape
    heads = width // HD
    rows = jnp.arange(here, dtype=jnp.int32) + lax.axis_index(axes) * here
    flags = needed_frames(rows, frame_slot, covisible, counts)
    q_all = lax.all_gather(queries, axes, axis=0, tiled=True)
    msg = attend(flags, q_all, keys, *prepare(keys, values)).astype(jnp.float32)
    top = msg[:, width : width + heads]
    totals = msg[:, width + heads : width + 2 * heads]
    factor = jnp.exp2(top - lax.pmax(top, axes))
    numer = msg[:, :width] * jnp.repeat(factor, HD, axis=1)
    own_numer = lax.psum_scatter(numer, axes, scatter_dimension=0, tiled=True)
    own_totals = lax.psum_scatter(totals * factor, axes, scatter_dimension=0, tiled=True)
    attended = (own_numer / jnp.repeat(own_totals, HD, axis=1)).astype(jnp.bfloat16)
    return jnp.dot(attended, out_weight, preferred_element_type=jnp.float32).astype(jnp.bfloat16)


def solution(mesh):
    group, dev = mesh.shape["group"], mesh.shape["dev"]
    body = body_any
    if group == 4 and dev == 8:
        body = functools.partial(body_cores, group * dev)
    return jax.shard_map(
        body,
        mesh=mesh,
        in_specs=(
            P(("group", "dev"), None),
            P(("group", "dev"), None, None),
            P(("group", "dev"), None, None),
            P(),
            P(),
            P(),
            P(),
        ),
        out_specs=P(("group", "dev"), None),
        check_vma=False,
    )
```

```python
import functools

import jax
import jax.numpy as jnp
from jax import lax
from jax.experimental import pallas as pl
from jax.experimental.pallas import tpu as pltpu
from jax.sharding import PartitionSpec as P

HD = 64
NEG_FILL = -1e30
LOG2E = 1.4426950408889634
MESH = pl.DeviceIdType.MESH
STAT = 128
TOP_STEP = 8.0
SMALL = 60.0
VMEM_LIMIT = 28 * 1024 * 1024
GATHER_VMEM_LIMIT = 56 * 1024 * 1024


def head_lanes(width):
    row_id = lax.broadcasted_iota(jnp.int32, (width, 128), 0)
    col_id = lax.broadcasted_iota(jnp.int32, (width, 128), 1)
    return jnp.where(lax.div(row_id, HD) == col_id, 1.0, 0.0).astype(jnp.bfloat16)


def largest_square(block, by_head):
    squares = jnp.dot(block * block, by_head, preferred_element_type=jnp.float32)
    return jnp.max(squares, axis=0, keepdims=True)


def turn_values(block, put, heads):
    turned = block.T
    for h in range(heads):
        put(h, slice(0, HD), turned[h * HD : (h + 1) * HD, :])
        put(h, slice(HD, HD + 16), jnp.ones((16, block.shape[0]), block.dtype))


def attend_kernel(flags, q_ref, k_ref, vt, ks_ref, out_ref, qt, acc, stat, wanted, *, heads, frames, tok, qframes):
    width = heads * HD
    scale = LOG2E * HD ** (-0.5)

    by_head = head_lanes(width)
    key_square = ks_ref[0:1, :]
    stat[...] = jnp.zeros_like(stat)
    qt[...] = jnp.zeros_like(qt)

    def one_query(qi, carry):
        rows = pl.ds(pl.multiple_of(qi * tok, tok), tok)
        for g in range(heads // 2):
            pair = q_ref[rows, g * 128 : (g + 1) * 128].T
            pair = pair * jnp.asarray(HD ** (-0.5), pair.dtype)
            qt[2 * g, 0:HD, :] = pair[0:HD, :]
            qt[2 * g + 1, HD:128, :] = pair[HD:128, :]
        acc[...] = jnp.zeros_like(acc)
        stat[0:heads, :] = jnp.full((heads, tok), NEG_FILL, jnp.float32)
        bound = jnp.max(largest_square(q_ref[rows, :], by_head) * key_square) * (scale * scale)
        small = bound <= SMALL * SMALL

        def scores(f, h):
            kp = k_ref[f, :, (h // 2) * 128 : (h // 2 + 1) * 128]
            return jnp.dot(kp, qt[h], preferred_element_type=jnp.float32)

        def small_frames(fs):
            stat[0:heads, :] = jnp.zeros((heads, tok), jnp.float32)
            tiles = [(f, h) for f in fs for h in range(heads)]

            def weigh(s):
                return jnp.exp(s).astype(jnp.bfloat16)

            def add(tile, p):
                f, h = tile
                acc[h] += jnp.dot(vt[f, h], p, preferred_element_type=jnp.float32)

            s, p = scores(*tiles[0]), None
            for t in range(len(tiles)):
                later = scores(*tiles[t + 1]) if t + 1 < len(tiles) else None
                now = weigh(s)
                if t > 0:
                    add(tiles[t - 1], p)
                s, p = later, now
            add(tiles[-1], p)

        def any_frame(f):
            for h in range(heads):
                s = scores(f, h)
                top = jnp.max(s, axis=0, keepdims=True) * LOG2E
                old = stat[h : h + 1, :]
                new = jnp.maximum(old, jnp.ceil(top * (1.0 / TOP_STEP)) * TOP_STEP)
                p = jnp.exp2(s * LOG2E - new).astype(jnp.bfloat16)
                add = jnp.dot(vt[f, h], p, preferred_element_type=jnp.float32)
                acc[h] = acc[h] * jnp.exp2(old - new) + add
                stat[h : h + 1, :] = new

        number = jnp.int32(0)
        for f in range(frames):
            wanted[number] = f
            number = number + flags[qi, f]

        @pl.when(small)
        def _():
            def two(i, c):
                small_frames([wanted[2 * i], wanted[2 * i + 1]])
                return c

            lax.fori_loop(0, lax.div(number, 2), two, 0)
            pl.when(lax.rem(number, 2) == 1)(lambda: small_frames([wanted[number - 1]]))

        @pl.when(jnp.logical_not(small))
        def _():
            def one(i, c):
                any_frame(wanted[i])
                return c

            lax.fori_loop(0, number, one, 0)

        for h in range(heads):
            stat[heads + h : heads + h + 1, :] = acc[h, HD : HD + 1, :]
        stats = jnp.concatenate([stat[...]] * (STAT // (2 * heads)), axis=0)
        for g in range(heads // 2):
            both = jnp.concatenate([acc[2 * g, 0:HD, :], acc[2 * g + 1, 0:HD, :]], axis=0)
            out_ref[rows, g * 128 : (g + 1) * 128] = both.astype(jnp.bfloat16).T
        out_ref[rows, width : width + STAT] = stats.astype(jnp.bfloat16).T
        return carry

    lax.fori_loop(0, qframes, one_query, 0)


def attend(flags, q, k, vt, key_square):
    rows, width = q.shape
    frames, tok = k.shape[0], k.shape[1]
    heads = width // HD
    qframes = rows // tok
    return pl.pallas_call(
        functools.partial(attend_kernel, heads=heads, frames=frames, tok=tok, qframes=qframes),
        out_shape=jax.ShapeDtypeStruct((rows, width + STAT), jnp.bfloat16),
        in_specs=[pl.BlockSpec(memory_space=pltpu.SMEM)] + [pl.BlockSpec(memory_space=pltpu.VMEM)] * 4,
        out_specs=pl.BlockSpec(memory_space=pltpu.VMEM),
        scratch_shapes=[
            pltpu.VMEM((heads, 128, tok), jnp.bfloat16),
            pltpu.VMEM((heads, HD + 16, tok), jnp.float32),
            pltpu.VMEM((2 * heads, tok), jnp.float32),
            pltpu.SMEM((frames + 1,), jnp.int32),
        ],
        compiler_params=pltpu.CompilerParams(vmem_limit_bytes=VMEM_LIMIT),
        name="attend",
    )(flags, q, k, vt, key_square)


def prepare_kernel(k_ref, v_ref, vt, ks_ref, *, heads, frames):
    by_head = head_lanes(k_ref.shape[2])

    def one(f, largest):
        def put(h, part, block):
            vt[f, h, part, :] = block

        turn_values(v_ref[f], put, heads)
        return jnp.maximum(largest, largest_square(k_ref[f], by_head))

    largest = lax.fori_loop(0, frames, one, jnp.zeros((1, 128), jnp.float32))
    ks_ref[...] = jnp.broadcast_to(largest, ks_ref.shape)


def prepare(k, v):
    frames, tok, width = k.shape
    heads = width // HD
    return pl.pallas_call(
        functools.partial(prepare_kernel, heads=heads, frames=frames),
        out_shape=(
            jax.ShapeDtypeStruct((frames, heads, HD + 16, tok), v.dtype),
            jax.ShapeDtypeStruct((8, 128), jnp.float32),
        ),
        compiler_params=pltpu.CompilerParams(vmem_limit_bytes=VMEM_LIMIT),
        name="prepare",
    )(k, v)


class Place:
    def __init__(self, nz):
        g, d = lax.axis_index("group"), lax.axis_index("dev")
        self.nz = nz
        self.y, self.c = lax.div(g, 2), lax.rem(g, 2)
        self.z, self.x = lax.div(d, 2), lax.rem(d, 2)
        self.other = (self.y * 2 + 1 - self.c, d)
        self.over_x = (g, self.z * 2 + 1 - self.x)
        self.over_y = ((1 - self.y) * 2 + self.c, d)
        self.up = (g, (self.z + 1) * 2 + self.x)
        self.down = (g, (self.z - 1) * 2 + self.x)
        self.has_up = self.z + 1 < nz
        self.has_down = self.z > 0

    def owner(self, p, x, y, z):
        return ((y * 2 + p) * self.nz + z) * 2 + x

    def greet(self):
        barrier = pltpu.get_barrier_semaphore()

        def tell(to):
            pl.semaphore_signal(barrier, inc=1, device_id=to, device_id_type=MESH)

        tell(self.other)
        tell(self.over_x)
        tell(self.over_y)
        pl.when(self.has_up)(lambda: tell(self.up))
        pl.when(self.has_down)(lambda: tell(self.down))
        peers = 3 + jnp.where(self.has_up, 1, 0) + jnp.where(self.has_down, 1, 0)
        pl.semaphore_wait(barrier, peers)


def remote(src, dst, send, recv, to):
    return pltpu.make_async_remote_copy(
        src_ref=src, dst_ref=dst, send_sem=send, recv_sem=recv, device_id=to, device_id_type=MESH
    )


def gather_kernel(
    slot_in, cov_in, count_in, q_in, k_in, v_in, q_all, k_all, vt, ks, flags, v_all, parcel, arrive, s_up, s_down, s_x, s_y, s_two, s_near, r_near, s_own, s_load, *, nz
):
    me = Place(nz)
    half = q_all.shape[2]
    here = k_in.shape[0]
    keep = pl.ds(pl.multiple_of(me.c * half, half), half)
    give = pl.ds(pl.multiple_of((1 - me.c) * half, half), half)
    mine = pl.ds(me.c * here, here)
    own = me.owner(me.c, me.x, me.y, me.z)
    own_copies = [
        pltpu.make_async_copy(q_in.at[:, keep], q_all.at[own], s_own.at[0]),
        pltpu.make_async_copy(k_in.at[:, :, keep], k_all.at[mine], s_own.at[1]),
        pltpu.make_async_copy(v_in.at[:, :, keep], v_all.at[mine], s_own.at[2]),
    ]
    steps = 2 * nz - 2
    near = []
    for t in range(2 * here):
        to_slot = (k_all, v_all)[t // here].at[me.c * here + t % here]
        near.append(remote(parcel.at[t], to_slot, s_near.at[1 + t], r_near.at[t], me.other))
    own_copies[0].start()
    loads = []
    for t in range(2 * here):
        src = (k_in, v_in)[t // here]
        loads.append(pltpu.make_async_copy(src.at[t % here, :, give], parcel.at[t], s_load.at[t]))
        loads[t].start()
    own_copies[1].start()
    own_copies[2].start()
    me.greet()
    heads = half // HD
    by_head = head_lanes(half)
    near_q = remote(q_in.at[:, give], q_all.at[own], s_near.at[0], arrive.at[own], me.other)
    near_q.start()
    own_copies[0].wait()

    def await_block(idx):
        remote(q_all.at[idx], q_all.at[idx], s_near.at[0], arrive.at[idx], me.over_x).wait_recv()

    def spread(p, i, off, zs):
        idx = me.owner(p, me.x, me.y, zs)
        blk = q_all.at[idx]
        up = remote(blk, blk, s_up.at[p, i], arrive.at[idx], me.up)
        down = remote(blk, blk, s_down.at[p, i], arrive.at[idx], me.down)
        return (
            (jnp.logical_and(off >= 0, me.has_up), up),
            (jnp.logical_and(off <= 0, me.has_down), down),
            (None, remote(blk, blk, s_x.at[p, i], arrive.at[idx], me.over_x)),
            (None, remote(blk, blk, s_y.at[p, i], arrive.at[idx], me.over_y)),
        )

    def begin(copies):
        for cond, copy in copies:
            if cond is None:
                copy.start()
            else:
                pl.when(cond)(copy.start)

    def sent(copies):
        for cond, copy in copies:
            if cond is None:
                copy.wait_send()
            else:
                pl.when(cond)(copy.wait_send)

    begin(spread(me.c, 0, jnp.int32(0), me.z))
    await_block(me.owner(1 - me.c, me.x, me.y, me.z))
    begin(spread(1 - me.c, 0, jnp.int32(0), me.z))

    def source(i):
        off = lax.div(i + 1, 2) * (2 * lax.rem(i, 2) - 1)
        zs = me.z - off
        return off, zs, jnp.logical_and(zs >= 0, zs < nz)

    def second(i, zs):
        a = me.owner(0, 1 - me.x, me.y, zs)
        b = me.owner(1, me.x, 1 - me.y, zs)
        return (
            (a, remote(q_all.at[a], q_all.at[a], s_two.at[0, i], arrive.at[a], me.over_y)),
            (b, remote(q_all.at[b], q_all.at[b], s_two.at[1, i], arrive.at[b], me.over_x)),
        )

    def do_second(i):
        off, zs, ok = source(i)

        @pl.when(ok)
        def _():
            for idx, copy in second(i, zs):
                await_block(idx)
                copy.start()

    def step(i, carry):
        off, zs, ok = source(i)

        @pl.when(ok)
        def _():
            for p in (0, 1):
                await_block(me.owner(p, me.x, me.y, zs))
                begin(spread(p, i, off, zs))

        do_second(i - 1)
        for t in range(2 * here):

            @pl.when(i == 1 + t * steps // (2 * here))
            def _():
                loads[t].wait()
                near[t].start()

        return carry

    count = 2 * nz - 1
    lax.fori_loop(1, count, step, 0)
    do_second(jnp.int32(count - 1))

    def finish(i, carry):
        off, zs, ok = source(i)

        @pl.when(ok)
        def _():
            await_block(me.owner(0, me.x, 1 - me.y, zs))
            await_block(me.owner(1, 1 - me.x, me.y, zs))
            await_block(me.owner(0, 1 - me.x, 1 - me.y, zs))
            await_block(me.owner(1, 1 - me.x, 1 - me.y, zs))
            for p in (0, 1):
                sent(spread(p, i, off, zs))
            for _, copy in second(i, zs):
                copy.wait_send()

        return carry

    slot_id = lax.broadcasted_iota(jnp.int32, cov_in.shape, 1)
    query_id = lax.broadcasted_iota(jnp.int32, cov_in.shape, 0)
    used = jnp.zeros(cov_in.shape, jnp.int32)
    for q in range(cov_in.shape[0]):
        used = jnp.where(query_id == q, count_in[q], used)
    listed = slot_id < used
    frame_id = lax.broadcasted_iota(jnp.int32, slot_in.shape, 1)
    lane = lax.broadcasted_iota(jnp.int32, flags.shape, 1)
    found = jnp.zeros(flags.shape, jnp.int32)
    for r in range(2 * here):
        row = ((me.y * 2 + r // here) * nz + me.z) * 2 * here + me.x * here + r % here
        frame = jnp.sum(jnp.where(slot_in[...] == row, frame_id, 0), axis=1, keepdims=True)
        hit = jnp.where(jnp.logical_and(cov_in[...] == frame, listed), 1, 0)
        found = found + jnp.where(lane == r, jnp.max(hit, axis=1, keepdims=True), 0)
    flags[...] = found

    def turn(core):
        def one(t, largest):
            f = core * here + t

            def put(h, part, block):
                vt[f, h, part, :] = block

            turn_values(v_all[f], put, heads)
            return jnp.maximum(largest, largest_square(k_all[f], by_head))

        return one

    own_copies[1].wait()
    own_copies[2].wait()
    largest = lax.fori_loop(0, here, turn(me.c), jnp.zeros((1, 128), jnp.float32))
    for copy in near:
        copy.wait()
    largest = lax.fori_loop(0, here, turn(1 - me.c), largest)
    ks[...] = jnp.broadcast_to(largest, ks.shape)
    lax.fori_loop(0, count, finish, 0)
    near_q.wait_send()


def gather(frame_slot, covisible, counts, q, k, v, devices):
    rows, width = q.shape
    frames, tok, _ = k.shape
    nz = devices // 8
    half = width // 2
    count = 2 * nz - 1
    dma = pltpu.SemaphoreType.DMA
    anywhere = pl.BlockSpec(memory_space=pl.ANY)
    vmem = pl.BlockSpec(memory_space=pltpu.VMEM)
    return pl.pallas_call(
        functools.partial(gather_kernel, nz=nz),
        out_shape=(
            jax.ShapeDtypeStruct((devices, rows, half), q.dtype),
            jax.ShapeDtypeStruct((2 * frames, tok, half), k.dtype),
            jax.ShapeDtypeStruct((2 * frames, half // HD, HD + 16, tok), v.dtype),
            jax.ShapeDtypeStruct((8, 128), jnp.float32),
            jax.ShapeDtypeStruct((covisible.shape[0], 2 * frames), jnp.int32),
        ),
        in_specs=[vmem, vmem, pl.BlockSpec(memory_space=pltpu.SMEM), vmem, anywhere, anywhere],
        out_specs=(vmem,) * 5,
        scratch_shapes=[
            pltpu.VMEM((2 * frames, tok, half), v.dtype),
            pltpu.VMEM((2 * frames, tok, half), k.dtype),
            dma((devices,)),
            dma((2, count)),
            dma((2, count)),
            dma((2, count)),
            dma((2, count)),
            dma((2, count)),
            dma((1 + 2 * frames,)),
            dma((2 * frames,)),
            dma((3,)),
            dma((2 * frames,)),
        ],
        compiler_params=pltpu.CompilerParams(
            collective_id=0, has_side_effects=True, vmem_limit_bytes=GATHER_VMEM_LIMIT
        ),
        name="gather",
    )(frame_slot[None, :], covisible, counts, q, k, v)


def expander(heads, first, width):
    r = lax.broadcasted_iota(jnp.int32, (STAT, width), 0)
    col = lax.broadcasted_iota(jnp.int32, (STAT, width), 1)
    in_stat = lax.rem(jnp.maximum(col - heads * HD, 0), 2 * heads) - heads
    head = jnp.where(col < heads * HD, lax.div(col, HD), in_stat)
    head = jnp.where(head < 0, -STAT, jnp.where(head < heads, head, -STAT))
    return jnp.where(head + first == r, 1.0, 0.0).astype(jnp.bfloat16)


def scatter_kernel(
    msg, w_in, out, weight, halves, s_weight, r_one, r_two, r_up, r_down, b_two, b_z, kept, att, exp_ref, exp_tot, copies_of, b_stat, r_stat,
    s_stat, sem_stat, sem_one, sem_two, sem_up, sem_down, s_one, s_two, s_z, sem_last, *, nz, heads
):
    me = Place(nz)
    width = heads * HD
    rows = msg.shape[1]
    count = 2 * nz - 1
    load = pltpu.make_async_copy(w_in, weight, s_weight.at[0])
    load.start()
    exp_ref[...] = expander(heads, 0, width + STAT)
    exp_tot[...] = expander(heads, heads, width)
    r_id = lax.broadcasted_iota(jnp.int32, (STAT, STAT), 0)
    c_id = lax.broadcasted_iota(jnp.int32, (STAT, STAT), 1)
    same = lax.rem(r_id, 2 * heads) == lax.rem(c_id, 2 * heads)
    copies_of[...] = jnp.where(same, 1.0, 0.0).astype(jnp.bfloat16)
    lane = lax.broadcasted_iota(jnp.int32, (rows, STAT), 1)
    slot = lax.div(lane, 2 * heads)
    lane = lax.rem(lane, 2 * heads)

    def one_target(p, k, zd):
        if k == 0:
            return me.owner(p, 1 - me.x, 1 - me.y, zd)
        return me.owner(0, me.x, 1 - me.y, zd) if p == 0 else me.owner(1, 1 - me.x, me.y, zd)

    for p in (0, 1):
        packed = jnp.zeros((rows, STAT), jnp.float32)
        for k in (0, 1):
            for zd in range(nz):
                stats = msg[one_target(p, k, zd), :, width:].astype(jnp.float32)
                packed = jnp.where(slot == k * nz + zd, stats, packed)
        b_stat[p] = packed.astype(jnp.bfloat16)
    me.greet()
    stat_copies = [
        remote(b_stat.at[p], r_stat.at[p], s_stat.at[p], sem_stat.at[p], to)
        for p, to in ((0, me.over_y), (1, me.over_x))
    ]

    def joined(p, k, zd):
        picked = jnp.where(slot == k * nz + zd, r_stat[p].astype(jnp.float32), 0.0).astype(jnp.bfloat16)
        stats = jnp.dot(picked, copies_of[...], preferred_element_type=jnp.float32)
        return jnp.concatenate([r_one[p, k, zd].astype(jnp.float32), stats], axis=1)

    def target(i):
        off = lax.div(count - i, 2) * (1 - 2 * lax.rem(i, 2))
        zd = me.z + off
        return off, zd, jnp.logical_and(zd >= 0, zd < nz)

    def merge(parts):
        parts = [part.astype(jnp.float32) for part in parts]
        stats = [part[:, width:] for part in parts]
        top = functools.reduce(jnp.maximum, stats)
        total = None
        for part, st in zip(parts, stats):
            factor = jnp.exp2(st - top).astype(jnp.bfloat16)
            wide = jnp.dot(factor, exp_ref[...], preferred_element_type=jnp.float32)
            total = part * wide if total is None else total + part * wide
        tail = jnp.where(lane < heads, top, total[:, width:])
        return jnp.concatenate([total[:, :width], tail], axis=1)

    def ones(i, zd):
        return tuple(
            remote(
                msg.at[one_target(p, k, zd), :, 0:width],
                r_one.at[p, k, zd],
                s_one.at[p, k, zd],
                sem_one.at[p, k, zd],
                (me.over_y, me.over_x)[p],
            )
            for k in (0, 1)
            for p in (0, 1)
        )

    def first(i, carry):
        off, zd, ok = target(i)

        @pl.when(ok)
        def _():
            for copy in ones(i, zd):
                copy.start()

        return carry

    for copy in stat_copies:
        copy.start()
    lax.fori_loop(0, count, first, 0)
    for copy in stat_copies:
        copy.wait_recv()

    def twos(zd):
        return tuple(
            remote(b_two.at[p, zd], r_two.at[p, zd], s_two.at[p, zd], sem_two.at[p, zd], to)
            for p, to in ((0, me.over_x), (1, me.over_y))
        )

    def second(i):
        off, zd, ok = target(i)

        @pl.when(ok)
        def _():
            waits = ones(i, zd)
            copies = twos(zd)
            for p in (0, 1):
                waits[p].wait_recv()
                src = me.owner(0, 1 - me.x, me.y, zd) if p == 0 else me.owner(1, me.x, 1 - me.y, zd)
                b_two[p, zd] = merge([msg[src], joined(p, 0, zd)]).astype(jnp.bfloat16)
                copies[p].start()

    def z_copies(p, zd):
        return (
            remote(b_z.at[p, zd], r_up.at[p, zd], s_z.at[p, zd], sem_up.at[p, zd], me.up),
            remote(b_z.at[p, zd], r_down.at[p, zd], s_z.at[p, zd], sem_down.at[p, zd], me.down),
        )

    def third(i):
        off, zd, ok = target(i)

        @pl.when(ok)
        def _():
            waits = ones(i, zd)
            two = twos(zd)
            for p in (0, 1):
                up, down = z_copies(p, zd)
                waits[2 + p].wait_recv()
                two[p].wait_recv()
                here = merge([msg[me.owner(p, me.x, me.y, zd)], joined(p, 1, zd), r_two[p, zd]])
                kept[p] = here

                @pl.when(jnp.logical_and(off >= 0, me.has_down))
                def _():
                    up.wait_recv()
                    kept[p] = merge([kept[p], r_up[p, zd]])

                @pl.when(jnp.logical_and(off <= 0, me.has_up))
                def _():
                    down.wait_recv()
                    kept[p] = merge([kept[p], r_down[p, zd]])

                @pl.when(off != 0)
                def _():
                    b_z[p, zd] = kept[p].astype(jnp.bfloat16)

                pl.when(off > 0)(up.start)
                pl.when(off < 0)(down.start)

    def step(i, carry):
        second(i)
        pl.when(i > 0)(lambda: third(i - 1))
        return carry

    lax.fori_loop(0, count, step, 0)
    third(jnp.int32(count - 1))

    for p in (0, 1):
        full = kept[p]
        tail = full[:, width:]
        inverse = 1.0 / jnp.where(jnp.logical_and(lane >= heads, lane < 2 * heads), tail, 1.0)
        hi = inverse.astype(jnp.bfloat16)
        lo = (inverse - hi.astype(jnp.float32)).astype(jnp.bfloat16)
        wide = jnp.dot(hi, exp_tot[...], preferred_element_type=jnp.float32)
        wide = wide + jnp.dot(lo, exp_tot[...], preferred_element_type=jnp.float32)
        att[p] = (full[:, :width] * wide).astype(jnp.bfloat16)
    last = remote(att.at[1 - me.c], halves.at[me.c], sem_last.at[0], sem_last.at[1], me.other)
    last.start()
    halves[me.c] = att[me.c]

    def finish(i, carry):
        off, zd, ok = target(i)

        @pl.when(ok)
        def _():
            for copy in ones(i, zd):
                copy.wait_send()
            for copy in twos(zd):
                copy.wait_send()
            for p in (0, 1):
                up, down = z_copies(p, zd)
                pl.when(off > 0)(up.wait_send)
                pl.when(off < 0)(down.wait_send)

        return carry

    lax.fori_loop(0, count, finish, 0)
    for copy in stat_copies:
        copy.wait_send()
    load.wait()
    last.wait()
    rows_in = jnp.concatenate([halves[0], halves[1]], axis=1)
    out[...] = jnp.dot(rows_in, weight[...], preferred_element_type=jnp.float32).astype(out.dtype)


def scatter(msg, weight, heads):
    devices, rows, wide = msg.shape
    nz = devices // 8
    width = heads * HD
    dma = pltpu.SemaphoreType.DMA
    vmem = pl.BlockSpec(memory_space=pltpu.VMEM)
    block = (rows, wide)
    return pl.pallas_call(
        functools.partial(scatter_kernel, nz=nz, heads=heads),
        out_shape=jax.ShapeDtypeStruct((rows, weight.shape[1]), jnp.bfloat16),
        in_specs=[vmem, pl.BlockSpec(memory_space=pl.ANY)],
        out_specs=vmem,
        scratch_shapes=[
            pltpu.VMEM(weight.shape, weight.dtype),
            pltpu.VMEM((2, rows, width), jnp.bfloat16),
            dma((1,)),
            pltpu.VMEM((2, 2, nz, rows, width), jnp.bfloat16),
            pltpu.VMEM((2, nz) + block, jnp.bfloat16),
            pltpu.VMEM((2, nz) + block, jnp.bfloat16),
            pltpu.VMEM((2, nz) + block, jnp.bfloat16),
            pltpu.VMEM((2, nz) + block, jnp.bfloat16),
            pltpu.VMEM((2, nz) + block, jnp.bfloat16),
            pltpu.VMEM((2,) + block, jnp.float32),
            pltpu.VMEM((2, rows, width), jnp.bfloat16),
            pltpu.VMEM((STAT, wide), jnp.bfloat16),
            pltpu.VMEM((STAT, width), jnp.bfloat16),
            pltpu.VMEM((STAT, STAT), jnp.bfloat16),
            pltpu.VMEM((2, rows, STAT), jnp.bfloat16),
            pltpu.VMEM((2, rows, STAT), jnp.bfloat16),
            dma((2,)),
            dma((2,)),
            dma((2, 2, nz)),
            dma((2, nz)),
            dma((2, nz)),
            dma((2, nz)),
            dma((2, 2, nz)),
            dma((2, nz)),
            dma((2, nz)),
            dma((2,)),
        ],
        compiler_params=pltpu.CompilerParams(
            collective_id=1, has_side_effects=True, vmem_limit_bytes=VMEM_LIMIT
        ),
        name="scatter",
    )(msg, weight)


def needed_frames(rows, frame_slot, covisible, counts):
    frame_ids = jnp.arange(frame_slot.shape[0], dtype=jnp.int32)
    hits = frame_slot[None, :] == rows[:, None]
    frames = jnp.sum(jnp.where(hits, frame_ids[None, :], 0), axis=1)
    in_list = jnp.arange(covisible.shape[1], dtype=jnp.int32)[None, :] < counts[:, None]
    match = (covisible[:, :, None] == frames[None, None, :]) & in_list[:, :, None]
    return jnp.any(match, axis=1).astype(jnp.int32)


def body_cores(devices, queries, keys, values, frame_slot, covisible, counts, out_weight):
    here, tok, width = keys.shape
    heads = width // HD // 2
    q_all, k_all, vt, key_square, flags = gather(frame_slot, covisible, counts, queries, keys, values, devices)
    own = queries.shape[0]
    msg = attend(flags, q_all.reshape(devices * own, width // 2), k_all, vt, key_square)
    return scatter(msg.reshape(devices, own, -1), out_weight, heads)


def body_any(queries, keys, values, frame_slot, covisible, counts, out_weight):
    axes = ("group", "dev")
    here, tok, width = keys.shape
    heads = width // HD
    rows = jnp.arange(here, dtype=jnp.int32) + lax.axis_index(axes) * here
    flags = needed_frames(rows, frame_slot, covisible, counts)
    q_all = lax.all_gather(queries, axes, axis=0, tiled=True)
    msg = attend(flags, q_all, keys, *prepare(keys, values)).astype(jnp.float32)
    top = msg[:, width : width + heads]
    totals = msg[:, width + heads : width + 2 * heads]
    factor = jnp.exp2(top - lax.pmax(top, axes))
    numer = msg[:, :width] * jnp.repeat(factor, HD, axis=1)
    own_numer = lax.psum_scatter(numer, axes, scatter_dimension=0, tiled=True)
    own_totals = lax.psum_scatter(totals * factor, axes, scatter_dimension=0, tiled=True)
    attended = (own_numer / jnp.repeat(own_totals, HD, axis=1)).astype(jnp.bfloat16)
    return jnp.dot(attended, out_weight, preferred_element_type=jnp.float32).astype(jnp.bfloat16)


def solution(mesh):
    group, dev = mesh.shape["group"], mesh.shape["dev"]
    body = body_any
    if group == 4 and dev == 8:
        body = functools.partial(body_cores, group * dev)
    return jax.shard_map(
        body,
        mesh=mesh,
        in_specs=(
            P(("group", "dev"), None),
            P(("group", "dev"), None, None),
            P(("group", "dev"), None, None),
            P(),
            P(),
            P(),
            P(),
        ),
        out_specs=P(("group", "dev"), None),
        check_vma=False,
    )
```

```python
import functools

import jax
import jax.numpy as jnp
from jax import lax
from jax.experimental import pallas as pl
from jax.experimental.pallas import tpu as pltpu
from jax.sharding import PartitionSpec as P

HD = 64
NEG_FILL = -1e30
LOG2E = 1.4426950408889634
MESH = pl.DeviceIdType.MESH
STAT = 128
TOP_STEP = 8.0
SMALL = 60.0
VMEM_LIMIT = 56 * 1024 * 1024


def head_lanes(width):
    row_id = lax.broadcasted_iota(jnp.int32, (width, 128), 0)
    col_id = lax.broadcasted_iota(jnp.int32, (width, 128), 1)
    return jnp.where(lax.div(row_id, HD) == col_id, 1.0, 0.0).astype(jnp.bfloat16)


def largest_square(block, by_head):
    squares = jnp.dot(block * block, by_head, preferred_element_type=jnp.float32)
    return jnp.max(squares, axis=0, keepdims=True)


def turn_values(block, put, heads):
    turned = block.T
    for h in range(heads):
        put(h, slice(0, HD), turned[h * HD : (h + 1) * HD, :])
        put(h, slice(HD, HD + 16), jnp.ones((16, block.shape[0]), block.dtype))


def attend_kernel(flags, q_ref, k_ref, vt, ks_ref, out_ref, qt, acc, stat, wanted, *, heads, frames, tok, qframes):
    width = heads * HD
    scale = LOG2E * HD ** (-0.5)

    by_head = head_lanes(width)
    key_square = ks_ref[0:1, :]
    stat[...] = jnp.zeros_like(stat)
    qt[...] = jnp.zeros_like(qt)

    def one_query(qi, carry):
        rows = pl.ds(pl.multiple_of(qi * tok, tok), tok)
        for g in range(heads // 2):
            pair = q_ref[rows, g * 128 : (g + 1) * 128].T
            pair = pair * jnp.asarray(HD ** (-0.5), pair.dtype)
            qt[2 * g, 0:HD, :] = pair[0:HD, :]
            qt[2 * g + 1, HD:128, :] = pair[HD:128, :]
        acc[...] = jnp.zeros_like(acc)
        stat[0:heads, :] = jnp.full((heads, tok), NEG_FILL, jnp.float32)
        bound = jnp.max(largest_square(q_ref[rows, :], by_head) * key_square) * (scale * scale)
        small = bound <= SMALL * SMALL

        def scores(f, h):
            kp = k_ref[f, :, (h // 2) * 128 : (h // 2 + 1) * 128]
            return jnp.dot(kp, qt[h], preferred_element_type=jnp.float32)

        def small_frames(fs):
            stat[0:heads, :] = jnp.zeros((heads, tok), jnp.float32)
            tiles = [(f, h) for f in fs for h in range(heads)]

            def weigh(s):
                return jnp.exp(s).astype(jnp.bfloat16)

            def add(tile, p):
                f, h = tile
                acc[h] += jnp.dot(vt[f, h], p, preferred_element_type=jnp.float32)

            s, p = scores(*tiles[0]), None
            for t in range(len(tiles)):
                later = scores(*tiles[t + 1]) if t + 1 < len(tiles) else None
                now = weigh(s)
                if t > 0:
                    add(tiles[t - 1], p)
                s, p = later, now
            add(tiles[-1], p)

        def any_frame(f):
            for h in range(heads):
                s = scores(f, h)
                top = jnp.max(s, axis=0, keepdims=True) * LOG2E
                old = stat[h : h + 1, :]
                new = jnp.maximum(old, jnp.ceil(top * (1.0 / TOP_STEP)) * TOP_STEP)
                p = jnp.exp2(s * LOG2E - new).astype(jnp.bfloat16)
                add = jnp.dot(vt[f, h], p, preferred_element_type=jnp.float32)
                acc[h] = acc[h] * jnp.exp2(old - new) + add
                stat[h : h + 1, :] = new

        number = jnp.int32(0)
        for f in range(frames):
            wanted[number] = f
            number = number + flags[qi, f]

        @pl.when(small)
        def _():
            def two(i, c):
                small_frames([wanted[2 * i], wanted[2 * i + 1]])
                return c

            lax.fori_loop(0, lax.div(number, 2), two, 0)
            pl.when(lax.rem(number, 2) == 1)(lambda: small_frames([wanted[number - 1]]))

        @pl.when(jnp.logical_not(small))
        def _():
            def one(i, c):
                any_frame(wanted[i])
                return c

            lax.fori_loop(0, number, one, 0)

        for h in range(heads):
            stat[heads + h : heads + h + 1, :] = acc[h, HD : HD + 1, :]
        stats = jnp.concatenate([stat[...]] * (STAT // (2 * heads)), axis=0)
        for g in range(heads // 2):
            both = jnp.concatenate([acc[2 * g, 0:HD, :], acc[2 * g + 1, 0:HD, :]], axis=0)
            out_ref[rows, g * 128 : (g + 1) * 128] = both.astype(jnp.bfloat16).T
        out_ref[rows, width : width + STAT] = stats.astype(jnp.bfloat16).T
        return carry

    lax.fori_loop(0, qframes, one_query, 0)


def attend(flags, q, k, vt, key_square):
    rows, width = q.shape
    frames, tok = k.shape[0], k.shape[1]
    heads = width // HD
    qframes = rows // tok
    return pl.pallas_call(
        functools.partial(attend_kernel, heads=heads, frames=frames, tok=tok, qframes=qframes),
        out_shape=jax.ShapeDtypeStruct((rows, width + STAT), jnp.bfloat16),
        in_specs=[pl.BlockSpec(memory_space=pltpu.SMEM)] + [pl.BlockSpec(memory_space=pltpu.VMEM)] * 4,
        out_specs=pl.BlockSpec(memory_space=pltpu.VMEM),
        scratch_shapes=[
            pltpu.VMEM((heads, 128, tok), jnp.bfloat16),
            pltpu.VMEM((heads, HD + 16, tok), jnp.float32),
            pltpu.VMEM((2 * heads, tok), jnp.float32),
            pltpu.SMEM((frames + 1,), jnp.int32),
        ],
        compiler_params=pltpu.CompilerParams(vmem_limit_bytes=VMEM_LIMIT),
        name="attend",
    )(flags, q, k, vt, key_square)


def prepare_kernel(k_ref, v_ref, vt, ks_ref, *, heads, frames):
    by_head = head_lanes(k_ref.shape[2])

    def one(f, largest):
        def put(h, part, block):
            vt[f, h, part, :] = block

        turn_values(v_ref[f], put, heads)
        return jnp.maximum(largest, largest_square(k_ref[f], by_head))

    largest = lax.fori_loop(0, frames, one, jnp.zeros((1, 128), jnp.float32))
    ks_ref[...] = jnp.broadcast_to(largest, ks_ref.shape)


def prepare(k, v):
    frames, tok, width = k.shape
    heads = width // HD
    return pl.pallas_call(
        functools.partial(prepare_kernel, heads=heads, frames=frames),
        out_shape=(
            jax.ShapeDtypeStruct((frames, heads, HD + 16, tok), v.dtype),
            jax.ShapeDtypeStruct((8, 128), jnp.float32),
        ),
        compiler_params=pltpu.CompilerParams(vmem_limit_bytes=VMEM_LIMIT),
        name="prepare",
    )(k, v)


class Place:
    def __init__(self, nz):
        g, d = lax.axis_index("group"), lax.axis_index("dev")
        self.nz = nz
        self.y, self.c = lax.div(g, 2), lax.rem(g, 2)
        self.z, self.x = lax.div(d, 2), lax.rem(d, 2)
        self.other = (self.y * 2 + 1 - self.c, d)
        self.over_x = (g, self.z * 2 + 1 - self.x)
        self.over_y = ((1 - self.y) * 2 + self.c, d)
        self.up = (g, (self.z + 1) * 2 + self.x)
        self.down = (g, (self.z - 1) * 2 + self.x)
        self.has_up = self.z + 1 < nz
        self.has_down = self.z > 0

    def owner(self, p, x, y, z):
        return ((y * 2 + p) * self.nz + z) * 2 + x

    def greet(self):
        barrier = pltpu.get_barrier_semaphore()

        def tell(to):
            pl.semaphore_signal(barrier, inc=1, device_id=to, device_id_type=MESH)

        tell(self.other)
        tell(self.over_x)
        tell(self.over_y)
        pl.when(self.has_up)(lambda: tell(self.up))
        pl.when(self.has_down)(lambda: tell(self.down))
        peers = 3 + jnp.where(self.has_up, 1, 0) + jnp.where(self.has_down, 1, 0)
        pl.semaphore_wait(barrier, peers)


def remote(src, dst, send, recv, to):
    return pltpu.make_async_remote_copy(
        src_ref=src, dst_ref=dst, send_sem=send, recv_sem=recv, device_id=to, device_id_type=MESH
    )


def gather_kernel(
    slot_in, cov_in, count_in, q_in, k_in, v_in, q_all, k_all, vt, ks, flags, v_all, parcel, arrive, s_up, s_down, s_x, s_y, s_two, s_near, r_near, s_own, s_load, *, nz
):
    me = Place(nz)
    half = q_all.shape[2]
    here = k_in.shape[0]
    keep = pl.ds(pl.multiple_of(me.c * half, half), half)
    give = pl.ds(pl.multiple_of((1 - me.c) * half, half), half)
    mine = pl.ds(me.c * here, here)
    own = me.owner(me.c, me.x, me.y, me.z)
    own_copies = [
        pltpu.make_async_copy(q_in.at[:, keep], q_all.at[own], s_own.at[0]),
        pltpu.make_async_copy(k_in.at[:, :, keep], k_all.at[mine], s_own.at[1]),
        pltpu.make_async_copy(v_in.at[:, :, keep], v_all.at[mine], s_own.at[2]),
    ]
    steps = 2 * nz - 2
    near = []
    for t in range(2 * here):
        to_slot = (k_all, v_all)[t // here].at[me.c * here + t % here]
        near.append(remote(parcel.at[t], to_slot, s_near.at[1 + t], r_near.at[t], me.other))
    own_copies[0].start()
    loads = []
    for t in range(2 * here):
        src = (k_in, v_in)[t // here]
        loads.append(pltpu.make_async_copy(src.at[t % here, :, give], parcel.at[t], s_load.at[t]))
        loads[t].start()
    own_copies[1].start()
    own_copies[2].start()
    me.greet()
    heads = half // HD
    by_head = head_lanes(half)
    near_q = remote(q_in.at[:, give], q_all.at[own], s_near.at[0], arrive.at[own], me.other)
    near_q.start()
    own_copies[0].wait()

    def await_block(idx):
        remote(q_all.at[idx], q_all.at[idx], s_near.at[0], arrive.at[idx], me.over_x).wait_recv()

    def spread(p, i, off, zs):
        idx = me.owner(p, me.x, me.y, zs)
        blk = q_all.at[idx]
        up = remote(blk, blk, s_up.at[p, i], arrive.at[idx], me.up)
        down = remote(blk, blk, s_down.at[p, i], arrive.at[idx], me.down)
        return (
            (jnp.logical_and(off >= 0, me.has_up), up),
            (jnp.logical_and(off <= 0, me.has_down), down),
            (None, remote(blk, blk, s_x.at[p, i], arrive.at[idx], me.over_x)),
            (None, remote(blk, blk, s_y.at[p, i], arrive.at[idx], me.over_y)),
        )

    def begin(copies):
        for cond, copy in copies:
            if cond is None:
                copy.start()
            else:
                pl.when(cond)(copy.start)

    def sent(copies):
        for cond, copy in copies:
            if cond is None:
                copy.wait_send()
            else:
                pl.when(cond)(copy.wait_send)

    begin(spread(me.c, 0, jnp.int32(0), me.z))
    await_block(me.owner(1 - me.c, me.x, me.y, me.z))
    begin(spread(1 - me.c, 0, jnp.int32(0), me.z))

    def source(i):
        off = lax.div(i + 1, 2) * (2 * lax.rem(i, 2) - 1)
        zs = me.z - off
        return off, zs, jnp.logical_and(zs >= 0, zs < nz)

    def second(i, zs):
        a = me.owner(0, 1 - me.x, me.y, zs)
        b = me.owner(1, me.x, 1 - me.y, zs)
        return (
            (a, remote(q_all.at[a], q_all.at[a], s_two.at[0, i], arrive.at[a], me.over_y)),
            (b, remote(q_all.at[b], q_all.at[b], s_two.at[1, i], arrive.at[b], me.over_x)),
        )

    def do_second(i):
        off, zs, ok = source(i)

        @pl.when(ok)
        def _():
            for idx, copy in second(i, zs):
                await_block(idx)
                copy.start()

    def step(i, carry):
        off, zs, ok = source(i)

        @pl.when(ok)
        def _():
            for p in (0, 1):
                await_block(me.owner(p, me.x, me.y, zs))
                begin(spread(p, i, off, zs))

        do_second(i - 1)
        for t in range(2 * here):

            @pl.when(i == 1 + t * steps // (2 * here))
            def _():
                loads[t].wait()
                near[t].start()

        return carry

    count = 2 * nz - 1
    lax.fori_loop(1, count, step, 0)
    do_second(jnp.int32(count - 1))

    def finish(i, carry):
        off, zs, ok = source(i)

        @pl.when(ok)
        def _():
            await_block(me.owner(0, me.x, 1 - me.y, zs))
            await_block(me.owner(1, 1 - me.x, me.y, zs))
            await_block(me.owner(0, 1 - me.x, 1 - me.y, zs))
            await_block(me.owner(1, 1 - me.x, 1 - me.y, zs))
            for p in (0, 1):
                sent(spread(p, i, off, zs))
            for _, copy in second(i, zs):
                copy.wait_send()

        return carry

    slot_id = lax.broadcasted_iota(jnp.int32, cov_in.shape, 1)
    query_id = lax.broadcasted_iota(jnp.int32, cov_in.shape, 0)
    used = jnp.zeros(cov_in.shape, jnp.int32)
    for q in range(cov_in.shape[0]):
        used = jnp.where(query_id == q, count_in[q], used)
    listed = slot_id < used
    frame_id = lax.broadcasted_iota(jnp.int32, slot_in.shape, 1)
    lane = lax.broadcasted_iota(jnp.int32, flags.shape, 1)
    found = jnp.zeros(flags.shape, jnp.int32)
    for r in range(2 * here):
        row = ((me.y * 2 + r // here) * nz + me.z) * 2 * here + me.x * here + r % here
        frame = jnp.sum(jnp.where(slot_in[...] == row, frame_id, 0), axis=1, keepdims=True)
        hit = jnp.where(jnp.logical_and(cov_in[...] == frame, listed), 1, 0)
        found = found + jnp.where(lane == r, jnp.max(hit, axis=1, keepdims=True), 0)
    flags[...] = found

    def turn(core):
        def one(t, largest):
            f = core * here + t

            def put(h, part, block):
                vt[f, h, part, :] = block

            turn_values(v_all[f], put, heads)
            return jnp.maximum(largest, largest_square(k_all[f], by_head))

        return one

    own_copies[1].wait()
    own_copies[2].wait()
    largest = lax.fori_loop(0, here, turn(me.c), jnp.zeros((1, 128), jnp.float32))
    for copy in near:
        copy.wait()
    largest = lax.fori_loop(0, here, turn(1 - me.c), largest)
    ks[...] = jnp.broadcast_to(largest, ks.shape)
    lax.fori_loop(0, count, finish, 0)
    near_q.wait_send()


def gather(frame_slot, covisible, counts, q, k, v, devices):
    rows, width = q.shape
    frames, tok, _ = k.shape
    nz = devices // 8
    half = width // 2
    count = 2 * nz - 1
    dma = pltpu.SemaphoreType.DMA
    anywhere = pl.BlockSpec(memory_space=pl.ANY)
    vmem = pl.BlockSpec(memory_space=pltpu.VMEM)
    return pl.pallas_call(
        functools.partial(gather_kernel, nz=nz),
        out_shape=(
            jax.ShapeDtypeStruct((devices, rows, half), q.dtype),
            jax.ShapeDtypeStruct((2 * frames, tok, half), k.dtype),
            jax.ShapeDtypeStruct((2 * frames, half // HD, HD + 16, tok), v.dtype),
            jax.ShapeDtypeStruct((8, 128), jnp.float32),
            jax.ShapeDtypeStruct((covisible.shape[0], 2 * frames), jnp.int32),
        ),
        in_specs=[vmem, vmem, pl.BlockSpec(memory_space=pltpu.SMEM), vmem, anywhere, anywhere],
        out_specs=(vmem,) * 5,
        scratch_shapes=[
            pltpu.VMEM((2 * frames, tok, half), v.dtype),
            pltpu.VMEM((2 * frames, tok, half), k.dtype),
            dma((devices,)),
            dma((2, count)),
            dma((2, count)),
            dma((2, count)),
            dma((2, count)),
            dma((2, count)),
            dma((1 + 2 * frames,)),
            dma((2 * frames,)),
            dma((3,)),
            dma((2 * frames,)),
        ],
        compiler_params=pltpu.CompilerParams(
            collective_id=0, has_side_effects=True, vmem_limit_bytes=VMEM_LIMIT
        ),
        name="gather",
    )(frame_slot[None, :], covisible, counts, q, k, v)


def expander(heads, first, width):
    r = lax.broadcasted_iota(jnp.int32, (STAT, width), 0)
    col = lax.broadcasted_iota(jnp.int32, (STAT, width), 1)
    in_stat = lax.rem(jnp.maximum(col - heads * HD, 0), 2 * heads) - heads
    head = jnp.where(col < heads * HD, lax.div(col, HD), in_stat)
    head = jnp.where(head < 0, -STAT, jnp.where(head < heads, head, -STAT))
    return jnp.where(head + first == r, 1.0, 0.0).astype(jnp.bfloat16)


def scatter_kernel(
    msg, w_in, out, weight, halves, s_weight, r_one, r_two, r_up, r_down, b_two, b_z, kept, att, exp_ref, exp_tot, copies_of, b_stat, r_stat,
    s_stat, sem_stat, sem_one, sem_two, sem_up, sem_down, s_one, s_two, s_z, sem_last, *, nz, heads
):
    me = Place(nz)
    width = heads * HD
    rows = msg.shape[1]
    count = 2 * nz - 1
    load = pltpu.make_async_copy(w_in, weight, s_weight.at[0])
    load.start()
    exp_ref[...] = expander(heads, 0, width + STAT)
    exp_tot[...] = expander(heads, heads, width)
    r_id = lax.broadcasted_iota(jnp.int32, (STAT, STAT), 0)
    c_id = lax.broadcasted_iota(jnp.int32, (STAT, STAT), 1)
    same = lax.rem(r_id, 2 * heads) == lax.rem(c_id, 2 * heads)
    copies_of[...] = jnp.where(same, 1.0, 0.0).astype(jnp.bfloat16)
    lane = lax.broadcasted_iota(jnp.int32, (rows, STAT), 1)
    slot = lax.div(lane, 2 * heads)
    lane = lax.rem(lane, 2 * heads)

    def one_target(p, k, zd):
        if k == 0:
            return me.owner(p, 1 - me.x, 1 - me.y, zd)
        return me.owner(0, me.x, 1 - me.y, zd) if p == 0 else me.owner(1, 1 - me.x, me.y, zd)

    for p in (0, 1):
        packed = jnp.zeros((rows, STAT), jnp.float32)
        for k in (0, 1):
            for zd in range(nz):
                stats = msg[one_target(p, k, zd), :, width:].astype(jnp.float32)
                packed = jnp.where(slot == k * nz + zd, stats, packed)
        b_stat[p] = packed.astype(jnp.bfloat16)
    me.greet()
    stat_copies = [
        remote(b_stat.at[p], r_stat.at[p], s_stat.at[p], sem_stat.at[p], to)
        for p, to in ((0, me.over_y), (1, me.over_x))
    ]

    def joined(p, k, zd):
        picked = jnp.where(slot == k * nz + zd, r_stat[p].astype(jnp.float32), 0.0).astype(jnp.bfloat16)
        stats = jnp.dot(picked, copies_of[...], preferred_element_type=jnp.float32)
        return jnp.concatenate([r_one[p, k, zd].astype(jnp.float32), stats], axis=1)

    def target(i):
        off = lax.div(count - i, 2) * (1 - 2 * lax.rem(i, 2))
        zd = me.z + off
        return off, zd, jnp.logical_and(zd >= 0, zd < nz)

    def merge(parts):
        parts = [part.astype(jnp.float32) for part in parts]
        stats = [part[:, width:] for part in parts]
        top = functools.reduce(jnp.maximum, stats)
        total = None
        for part, st in zip(parts, stats):
            factor = jnp.exp2(st - top).astype(jnp.bfloat16)
            wide = jnp.dot(factor, exp_ref[...], preferred_element_type=jnp.float32)
            total = part * wide if total is None else total + part * wide
        tail = jnp.where(lane < heads, top, total[:, width:])
        return jnp.concatenate([total[:, :width], tail], axis=1)

    def ones(i, zd):
        return tuple(
            remote(
                msg.at[one_target(p, k, zd), :, 0:width],
                r_one.at[p, k, zd],
                s_one.at[p, k, zd],
                sem_one.at[p, k, zd],
                (me.over_y, me.over_x)[p],
            )
            for k in (0, 1)
            for p in (0, 1)
        )

    def first(i, carry):
        off, zd, ok = target(i)

        @pl.when(ok)
        def _():
            for copy in ones(i, zd):
                copy.start()

        return carry

    for copy in stat_copies:
        copy.start()
    lax.fori_loop(0, count, first, 0)
    for copy in stat_copies:
        copy.wait_recv()

    def twos(zd):
        return tuple(
            remote(b_two.at[p, zd], r_two.at[p, zd], s_two.at[p, zd], sem_two.at[p, zd], to)
            for p, to in ((0, me.over_x), (1, me.over_y))
        )

    def second(i):
        off, zd, ok = target(i)

        @pl.when(ok)
        def _():
            waits = ones(i, zd)
            copies = twos(zd)
            for p in (0, 1):
                waits[p].wait_recv()
                src = me.owner(0, 1 - me.x, me.y, zd) if p == 0 else me.owner(1, me.x, 1 - me.y, zd)
                b_two[p, zd] = merge([msg[src], joined(p, 0, zd)]).astype(jnp.bfloat16)
                copies[p].start()

    def z_copies(p, zd):
        return (
            remote(b_z.at[p, zd], r_up.at[p, zd], s_z.at[p, zd], sem_up.at[p, zd], me.up),
            remote(b_z.at[p, zd], r_down.at[p, zd], s_z.at[p, zd], sem_down.at[p, zd], me.down),
        )

    def third(i):
        off, zd, ok = target(i)

        @pl.when(ok)
        def _():
            waits = ones(i, zd)
            two = twos(zd)
            for p in (0, 1):
                up, down = z_copies(p, zd)
                waits[2 + p].wait_recv()
                two[p].wait_recv()
                here = merge([msg[me.owner(p, me.x, me.y, zd)], joined(p, 1, zd), r_two[p, zd]])
                kept[p] = here

                @pl.when(jnp.logical_and(off >= 0, me.has_down))
                def _():
                    up.wait_recv()
                    kept[p] = merge([kept[p], r_up[p, zd]])

                @pl.when(jnp.logical_and(off <= 0, me.has_up))
                def _():
                    down.wait_recv()
                    kept[p] = merge([kept[p], r_down[p, zd]])

                @pl.when(off != 0)
                def _():
                    b_z[p, zd] = kept[p].astype(jnp.bfloat16)

                pl.when(off > 0)(up.start)
                pl.when(off < 0)(down.start)

    def step(i, carry):
        second(i)
        pl.when(i > 0)(lambda: third(i - 1))
        return carry

    lax.fori_loop(0, count, step, 0)
    third(jnp.int32(count - 1))

    for p in (0, 1):
        full = kept[p]
        tail = full[:, width:]
        inverse = 1.0 / jnp.where(jnp.logical_and(lane >= heads, lane < 2 * heads), tail, 1.0)
        hi = inverse.astype(jnp.bfloat16)
        lo = (inverse - hi.astype(jnp.float32)).astype(jnp.bfloat16)
        wide = jnp.dot(hi, exp_tot[...], preferred_element_type=jnp.float32)
        wide = wide + jnp.dot(lo, exp_tot[...], preferred_element_type=jnp.float32)
        att[p] = (full[:, :width] * wide).astype(jnp.bfloat16)
    last = remote(att.at[1 - me.c], halves.at[me.c], sem_last.at[0], sem_last.at[1], me.other)
    last.start()
    halves[me.c] = att[me.c]

    def finish(i, carry):
        off, zd, ok = target(i)

        @pl.when(ok)
        def _():
            for copy in ones(i, zd):
                copy.wait_send()
            for copy in twos(zd):
                copy.wait_send()
            for p in (0, 1):
                up, down = z_copies(p, zd)
                pl.when(off > 0)(up.wait_send)
                pl.when(off < 0)(down.wait_send)

        return carry

    lax.fori_loop(0, count, finish, 0)
    for copy in stat_copies:
        copy.wait_send()
    load.wait()
    last.wait()
    rows_in = jnp.concatenate([halves[0], halves[1]], axis=1)
    out[...] = jnp.dot(rows_in, weight[...], preferred_element_type=jnp.float32).astype(out.dtype)


def scatter(msg, weight, heads):
    devices, rows, wide = msg.shape
    nz = devices // 8
    width = heads * HD
    dma = pltpu.SemaphoreType.DMA
    vmem = pl.BlockSpec(memory_space=pltpu.VMEM)
    block = (rows, wide)
    return pl.pallas_call(
        functools.partial(scatter_kernel, nz=nz, heads=heads),
        out_shape=jax.ShapeDtypeStruct((rows, weight.shape[1]), jnp.bfloat16),
        in_specs=[vmem, pl.BlockSpec(memory_space=pl.ANY)],
        out_specs=vmem,
        scratch_shapes=[
            pltpu.VMEM(weight.shape, weight.dtype),
            pltpu.VMEM((2, rows, width), jnp.bfloat16),
            dma((1,)),
            pltpu.VMEM((2, 2, nz, rows, width), jnp.bfloat16),
            pltpu.VMEM((2, nz) + block, jnp.bfloat16),
            pltpu.VMEM((2, nz) + block, jnp.bfloat16),
            pltpu.VMEM((2, nz) + block, jnp.bfloat16),
            pltpu.VMEM((2, nz) + block, jnp.bfloat16),
            pltpu.VMEM((2, nz) + block, jnp.bfloat16),
            pltpu.VMEM((2,) + block, jnp.float32),
            pltpu.VMEM((2, rows, width), jnp.bfloat16),
            pltpu.VMEM((STAT, wide), jnp.bfloat16),
            pltpu.VMEM((STAT, width), jnp.bfloat16),
            pltpu.VMEM((STAT, STAT), jnp.bfloat16),
            pltpu.VMEM((2, rows, STAT), jnp.bfloat16),
            pltpu.VMEM((2, rows, STAT), jnp.bfloat16),
            dma((2,)),
            dma((2,)),
            dma((2, 2, nz)),
            dma((2, nz)),
            dma((2, nz)),
            dma((2, nz)),
            dma((2, 2, nz)),
            dma((2, nz)),
            dma((2, nz)),
            dma((2,)),
        ],
        compiler_params=pltpu.CompilerParams(
            collective_id=1, has_side_effects=True, vmem_limit_bytes=VMEM_LIMIT
        ),
        name="scatter",
    )(msg, weight)


def needed_frames(rows, frame_slot, covisible, counts):
    frame_ids = jnp.arange(frame_slot.shape[0], dtype=jnp.int32)
    hits = frame_slot[None, :] == rows[:, None]
    frames = jnp.sum(jnp.where(hits, frame_ids[None, :], 0), axis=1)
    in_list = jnp.arange(covisible.shape[1], dtype=jnp.int32)[None, :] < counts[:, None]
    match = (covisible[:, :, None] == frames[None, None, :]) & in_list[:, :, None]
    return jnp.any(match, axis=1).astype(jnp.int32)


def body_cores(devices, queries, keys, values, frame_slot, covisible, counts, out_weight):
    here, tok, width = keys.shape
    heads = width // HD // 2
    q_all, k_all, vt, key_square, flags = gather(frame_slot, covisible, counts, queries, keys, values, devices)
    own = queries.shape[0]
    msg = attend(flags, q_all.reshape(devices * own, width // 2), k_all, vt, key_square)
    return scatter(msg.reshape(devices, own, -1), out_weight, heads)


def body_any(queries, keys, values, frame_slot, covisible, counts, out_weight):
    axes = ("group", "dev")
    here, tok, width = keys.shape
    heads = width // HD
    rows = jnp.arange(here, dtype=jnp.int32) + lax.axis_index(axes) * here
    flags = needed_frames(rows, frame_slot, covisible, counts)
    q_all = lax.all_gather(queries, axes, axis=0, tiled=True)
    msg = attend(flags, q_all, keys, *prepare(keys, values)).astype(jnp.float32)
    top = msg[:, width : width + heads]
    totals = msg[:, width + heads : width + 2 * heads]
    factor = jnp.exp2(top - lax.pmax(top, axes))
    numer = msg[:, :width] * jnp.repeat(factor, HD, axis=1)
    own_numer = lax.psum_scatter(numer, axes, scatter_dimension=0, tiled=True)
    own_totals = lax.psum_scatter(totals * factor, axes, scatter_dimension=0, tiled=True)
    attended = (own_numer / jnp.repeat(own_totals, HD, axis=1)).astype(jnp.bfloat16)
    return jnp.dot(attended, out_weight, preferred_element_type=jnp.float32).astype(jnp.bfloat16)


def solution(mesh):
    group, dev = mesh.shape["group"], mesh.shape["dev"]
    body = body_any
    if group == 4 and dev == 8:
        body = functools.partial(body_cores, group * dev)
    return jax.shard_map(
        body,
        mesh=mesh,
        in_specs=(
            P(("group", "dev"), None),
            P(("group", "dev"), None, None),
            P(("group", "dev"), None, None),
            P(),
            P(),
            P(),
            P(),
        ),
        out_specs=P(("group", "dev"), None),
        check_vma=False,
    )
```
